32 devices in a mesh: wide: 8 (over z, x), node: 4 (over y, core).
Axes of the slice: x: 2, y: 2, z: 4, core: 2. Of those that a mesh axis runs over, the one named last changes fastest.
Arguments:
- tokens: bfloat16 [4096, 12288], P(('wide', 'node')), may hold values from -6 to 6
- weight_codes: bfloat16 [12288, 128], P('wide', 'node'), may hold values from -4 to 4
- block_scales: bfloat16 [96, 128], P(None, 'node'), may hold values from 0.0029907227 to 0.029907227
- cotangent: bfloat16 [4096, 128], P(('wide', 'node')), may hold values from -0.09375 to 0.09375
Outputs:
- projected: bfloat16 [4096, 128], P(('wide', 'node'))
- weight_grad: float32 [12288, 128], P('wide', 'node')
The draws below stay inside these ranges and needn't reach their ends.
All inputs are finite; a program needn't handle non-finite values.
Results may differ from the reference program's by a relative error of at most 0.015.
Values may be sent and summed in bfloat16 or wider, within the bound.
No kernel may reach another device: no remote copies, remote signals or barrier semaphores. Data moves between devices by JAX's collectives and lax.ppermute only.
A program may use at most 64 MiB of HBM per device.

```python
import math
import jax
import jax.numpy as jnp
from jax import lax

D = 12288
K = 128
BLOCK = 128
TOK_DEV = 128
TOKENS = 4096
N_WIDE = 8
N_NODE = 4


def strengthened(entries, rng, source, target, shards_of, factor):
    def block_of(dim):
        return (jnp.arange(entries.shape[dim]) // (entries.shape[dim] // shards_of)).reshape((-1,) + (1,) * (entries.ndim - 1 - dim))

    first = jax.random.permutation(rng, shards_of)[block_of(target)]
    second = (block_of(target) + shards_of // 2) % shards_of
    return jnp.where((block_of(source) == first) | (block_of(source) == second), factor * entries, entries)


def steps_of(stream_key, extent, shards, low, top_value):
    def one(axis_at, shards_of):
        steps = jax.random.uniform(jax.random.fold_in(jax.random.fold_in(stream_key, 6), axis_at), (shards_of,), jnp.float32, low / len(shards), top_value / len(shards))
        return jnp.repeat(jnp.exp(steps), extent[axis_at] // shards_of).reshape((-1,) + (1,) * (len(extent) - axis_at - 1))

    factor_of = one(*shards[0])
    for cut in shards[1:]:
        factor_of = factor_of * one(*cut)
    return factor_of


def scatter_about(stream_key, shape, width, limit, split=(), kind=jnp.bfloat16):
    result = width * jax.random.normal(stream_key, shape, jnp.float32)
    if split:
        result = result * steps_of(stream_key, shape, split, -0.22, 0.18)
    return jnp.clip(result, -limit, limit).astype(kind)


def bell_draw_with(own_key, shape, deviation, limit, shards, heavy, kind=jnp.bfloat16):
    drawn = deviation * jax.random.normal(own_key, shape, jnp.float32)
    if shards:
        drawn = drawn * steps_of(own_key, shape, shards, -0.22, 0.18)
    return jnp.clip(strengthened(drawn, jax.random.fold_in(own_key, 3), *heavy), -limit, limit).astype(kind)


def setup_inputs(seed: int = 0) -> dict:
    keys = jax.random.split(jax.random.key(seed), 5)
    return {
        "tokens": bell_draw_with(keys[0], (TOKENS, D), 1.0, 6.0, ((0, 32),), (0, 1, 32, 2.75)),
        "weight_codes": scatter_about(keys[1], (D, K), 1.0, 4.0, ((0, 8), (1, 4))),
        "block_scales": jnp.clip(jnp.exp(math.log(0.029907227) - 2.3025851 * jax.random.uniform(keys[2], (D // BLOCK, K), jnp.float32) ** steps_of(keys[2], (D // BLOCK, K), ((1, 4),), -0.2, 0.2)), 0.0029907227, 0.029907227).astype(jnp.bfloat16),
        "cotangent": scatter_about(keys[3], (TOKENS, K), (TOKENS ** -0.5), 0.09375, ((0, 32),)),
    }


def reference(tokens, weight_codes, block_scales, cotangent):
    factor = jnp.repeat(block_scales.astype(jnp.float32), BLOCK, axis=0)
    weight = (weight_codes.astype(jnp.float32) * factor).astype(jnp.bfloat16)
    projected = jnp.dot(tokens, weight, preferred_element_type=jnp.float32).astype(jnp.bfloat16)
    token_blocks = tokens.reshape(N_WIDE, N_NODE, TOK_DEV, D)
    cot_blocks = cotangent.reshape(N_WIDE, N_NODE, TOK_DEV, K)

    def node_step(acc, pair):
        part = lax.dot_general(pair[0], pair[1], (((0,), (0,)), ((), ())), preferred_element_type=jnp.float32)
        part = lax.optimization_barrier(part.astype(jnp.bfloat16))
        return acc + part.astype(jnp.float32), None

    def wide_step(acc, pair):
        node_sum, unused = lax.scan(node_step, jnp.zeros((D, K), jnp.float32), pair)
        return acc + node_sum, None

    weight_grad, unused = lax.scan(wide_step, jnp.zeros((D, K), jnp.float32), (token_blocks, cot_blocks))
    return projected, weight_grad
```

```python
import functools

import jax
import jax.numpy as jnp
from jax import lax
from jax.experimental import pallas as pl
from jax.experimental.pallas import tpu as pltpu
from jax.sharding import PartitionSpec as P

BLOCK = 128
F32 = jnp.float32
BF16 = jnp.bfloat16
NT = (((1,), (1,)), ((), ()))
VMEM = pl.BlockSpec(memory_space=pltpu.VMEM)
ANY = pl.BlockSpec(memory_space=pl.ANY)
PARAMS = pltpu.CompilerParams(vmem_limit_bytes=10 << 20)


def place_of(h, x, y, ys):
    return 2 * (ys * x + y) + h


def turn_of(h, x, y, ys):
    if x and y:
        return 0, 2 * (y - 1) + h
    if (x and h) or (y and not h):
        return 0, 2 * (ys - 1) + y
    return 1, (2 + y if x or y else h)


def flip(entries, axis, offset, size):
    return lax.ppermute(entries, axis, [(i, i ^ offset) for i in range(size)])


def columns_of(x, z, cols):
    place = lax.bitwise_xor(lax.axis_index("wide"), 2 * z + x) * cols
    return pl.ds(pl.multiple_of(place, cols), cols)


def first_kernel(ys, zs, tokens, cot, codes, scales, *refs):
    (*made, weight, tokens_v, cot_v, codes_v, scales_v, cot_t, sems) = refs
    rows, cols = codes.shape
    half = cols // 2
    fetched = []

    def fetch(src, dst):
        fetched.append(pltpu.make_async_copy(src, dst, sems.at[len(fetched)]))
        fetched[-1].start()

    for src, dst in ((cot, cot_v), (codes, codes_v), (scales, scales_v)):
        fetch(src, dst)
    order = [(x, z) for x in (1, 0) for z in range(zs)]
    for x, z in order:
        place = columns_of(x, z, cols)
        fetch(tokens.at[:, place], tokens_v.at[:, place])
    for copy in fetched[:3]:
        copy.wait()

    blocks = cols // BLOCK
    first = lax.axis_index("wide") * blocks
    shape = (scales.shape[1], blocks)
    chosen = lax.broadcasted_iota(jnp.int32, shape, 0) == first + lax.broadcasted_iota(jnp.int32, shape, 1)
    factor = jnp.dot(scales_v[...], chosen.astype(F32).astype(BF16), preferred_element_type=F32)
    for b in range(blocks):
        at = b * BLOCK
        piece = (codes_v[:, at : at + BLOCK].astype(F32) * factor[:, b : b + 1]).astype(BF16)
        weight[at // half, :, at % half : at % half + BLOCK] = piece

    cot_t[...] = cot_v[...].astype(F32).T.astype(BF16)
    node = lax.axis_index("node")
    names = [(core, y) for core in (1, 0) for y in range(ys)]
    picked = []
    for core, y in names:
        place = lax.bitwise_xor(node, 2 * y + core) * rows
        picked.append(cot_t[pl.ds(pl.multiple_of(place, rows), rows), :])
    left = jnp.concatenate(picked, axis=0)
    for copy, (x, z) in zip(fetched[3:], order):
        copy.wait()
        right = tokens_v[:, columns_of(x, z, cols)]
        for h in range(2):
            part = jnp.dot(left, right[:, h * half : (h + 1) * half], preferred_element_type=F32).astype(BF16)
            for i, (core, y) in enumerate(names):
                turn, at = turn_of(h, x, y, ys)
                made[2 * (1 - core) + turn][at, z] = part[i * rows : (i + 1) * rows]


def local_products(tokens, cot, codes, scales, ys, zs):
    rows, cols = codes.shape
    half = cols // 2
    operands = (tokens, cot, codes, scales)
    blocks = [jax.ShapeDtypeStruct((n, zs, rows, half), BF16) for n in (3 * ys - 2, ys + 2)]
    return pl.pallas_call(
        functools.partial(first_kernel, ys, zs),
        out_shape=(*blocks, *blocks, jax.ShapeDtypeStruct((2, rows, half), BF16)),
        in_specs=[ANY] * 4,
        out_specs=(VMEM,) * 5,
        scratch_shapes=[pltpu.VMEM(a.shape, BF16) for a in operands]
        + [pltpu.VMEM(cot.shape[::-1], BF16), pltpu.SemaphoreType.DMA((3 + 2 * zs,))],
        compiler_params=PARAMS,
        cost_estimate=pl.CostEstimate(
            flops=2 * tokens.size * cot.shape[1], bytes_accessed=4 * tokens.size, transcendentals=0
        ),
        name="first",
    )(*[pltpu.with_memory_space_constraint(a, pltpu.HBM) for a in operands])


def plain_products(tokens, cot, codes, scales, ys, zs):
    rows, cols = codes.shape
    half = cols // 2
    node, wide = lax.axis_index("node"), lax.axis_index("wide")
    part = jnp.dot(cot.T, tokens, preferred_element_type=F32).astype(BF16)
    part = part.reshape(2 * ys, rows, 2 * zs, 2, half).transpose(3, 0, 2, 1, 4)
    part = jnp.take(part, jnp.arange(2 * ys) ^ node, axis=1)
    part = jnp.take(part, jnp.arange(2 * zs) ^ wide, axis=2)
    part = part.reshape(2, ys, 2, zs, 2, rows, half).transpose(2, 4, 1, 0, 3, 5, 6)
    part = part.reshape(2, 4 * ys, zs, rows, half)
    split = []
    for core in (1, 0):
        named = {turn_of(h, x, y, ys): part[core, place_of(h, x, y, ys)] for h in range(2) for x in range(2) for y in range(ys)}
        for turn, count in enumerate((3 * ys - 2, ys + 2)):
            split.append(jnp.stack([named[turn, i] for i in range(count)]))
    index = (wide * cols + jnp.arange(cols)) // BLOCK
    factor = jnp.take(scales, index, axis=1).astype(F32)
    weight = (codes.astype(F32) * factor).astype(BF16)
    weight = weight.reshape(rows, 2, half).transpose(1, 0, 2)
    return *split, weight


def add_up(outs, arrays, after=(), name="add_up", kind=BF16):
    shapes = [jax.ShapeDtypeStruct(shape, kind) for shape, _ in outs]
    rows, half = arrays[0].shape[-2:]
    if half % BLOCK or rows % 16:
        results = []
        for shape, places in outs:
            result = jnp.zeros(shape, kind)
            for at, terms in places:
                total = sum(arrays[a][i].astype(F32) for a, i in terms)
                result = result.at[at].set(total.astype(kind))
            results.append(result)
        return results

    def kernel(*refs):
        given, made = refs[: len(arrays)], refs[len(arrays) + len(after) :]
        for out, (_, places) in zip(made, outs):
            for at, terms in places:
                terms = [given[a][i] for a, i in terms]
                if len(terms) > 1:
                    terms = [sum(t.astype(F32) for t in terms).astype(kind)]
                out[at] = terms[0]

    return pl.pallas_call(
        kernel,
        out_shape=shapes,
        in_specs=[VMEM] * len(arrays) + [ANY] * len(after),
        out_specs=[VMEM] * len(outs),
        compiler_params=PARAMS,
        name=name,
    )(*arrays, *after)


def finish(sums, arrays, after):
    rows, half = arrays[0].shape[-2:]

    def total(given, h):
        return sum(given[a][i].astype(F32) for a, i in sums[h])

    if half % BLOCK or rows % 16:
        return jnp.concatenate([total(arrays, h) for h in range(2)], axis=1)

    def kernel(*refs):
        for h in range(2):
            refs[-1][:, h * half : (h + 1) * half] = total(refs[:-2], h)

    return pl.pallas_call(
        kernel,
        out_shape=jax.ShapeDtypeStruct((rows, 2 * half), F32),
        in_specs=[VMEM] * len(arrays) + [ANY],
        out_specs=VMEM,
        compiler_params=PARAMS,
        cost_estimate=pl.CostEstimate(flops=4 * 10**10, bytes_accessed=1, transcendentals=0),
        name="finish",
    )(*arrays, after)


def project_kernel(ys, zs, tokens, *refs):
    weights, out, total_t = refs[:4], refs[4], refs[5]
    rows, half = weights[0].shape[2:]
    cols = 2 * half
    most = 2 * ys + 2
    node = lax.axis_index("node")
    total = jnp.zeros((2 * ys * rows, tokens.shape[0]), F32)
    for x in range(2):
        for z in range(zs):
            pieces = tokens[:, columns_of(x, z, cols)]
            for h in range(2):
                picked = []
                for n in range(2 * ys):
                    at = place_of(h, x, n // 2, ys)
                    picked.append(weights[2 * (n % 2) + (at >= most)][at % most, z])
                left = jnp.concatenate(picked, axis=0)
                right = pieces[:, h * half : (h + 1) * half]
                total = total + lax.dot_general(left, right, NT, preferred_element_type=F32)
    total_t[...] = total.reshape(total_t.shape)
    ordered = [total_t[lax.bitwise_xor(node, n)] for n in range(2 * ys)]
    out[...] = jnp.concatenate(ordered, axis=0).T.astype(BF16)


def project(tokens, weights, ys, zs):
    rows = weights[0].shape[2]
    width = 2 * ys * rows
    return pl.pallas_call(
        functools.partial(project_kernel, ys, zs),
        out_shape=jax.ShapeDtypeStruct((tokens.shape[0], width), BF16),
        in_specs=[VMEM] * 5,
        out_specs=VMEM,
        scratch_shapes=[pltpu.VMEM((2 * ys, rows, tokens.shape[0]), F32)],
        compiler_params=PARAMS,
        cost_estimate=pl.CostEstimate(
            flops=2 * tokens.size * width, bytes_accessed=4 * tokens.size, transcendentals=0
        ),
        name="project",
    )(tokens, *weights)


def plain_project(tokens, weights, ys, zs):
    rows, half = weights[0].shape[2:]
    weights = [jnp.concatenate(weights[:2]), jnp.concatenate(weights[2:])]
    node, wide = lax.axis_index("node"), lax.axis_index("wide")
    pieces = tokens.reshape(tokens.shape[0], 2 * zs, 2, half)
    pieces = jnp.take(pieces, jnp.arange(2 * zs) ^ wide, axis=1)
    pieces = pieces.reshape(tokens.shape[0], zs, 2, 2, half)
    total = []
    for n in range(2 * ys):
        part = 0.0
        for h in range(2):
            for x in range(2):
                held = weights[n % 2][place_of(h, x, n // 2, ys)]
                part = part + jnp.einsum("tzl,zrl->tr", pieces[:, :, x, h], held, preferred_element_type=F32)
        total.append(part)
    total = jnp.take(jnp.stack(total, axis=1), jnp.arange(2 * ys) ^ node, axis=1)
    return total.reshape(tokens.shape[0], -1).astype(BF16)


def on_device(wides, nodes, tokens, codes, scales, cotangent):
    ys, zs = nodes // 2, wides // 2
    cols, rows = codes.shape
    half = cols // 2
    aligned = half % BLOCK == 0 and rows % 16 == 0
    products, make_project = (local_products, project) if aligned else (plain_products, plain_project)
    others = range(1, ys)
    one = (zs, rows, half)
    whole = (...,)

    def core_flip(entries):
        return flip(entries, "node", 1, nodes)

    def y_flip(entries, y):
        return flip(entries, "node", 2 * y, nodes)

    def x_flip(entries):
        return flip(entries, "wide", 1, wides)

    def z_flip(entries, z):
        return flip(entries, "wide", 2 * z, wides)

    sent0, sent1, kept0, kept1, weight = products(tokens, cotangent, codes.T, scales.T, ys, zs)

    got0, got1 = core_flip(sent0), core_flip(sent1)
    held = [weight, z_flip(weight, zs // 2)]
    offsets = [0, zs // 2]
    places = [(0, ()), (1, ())]

    def pair(h, x, y):
        _, at = turn_of(h, x, y, ys)
        return [(0, (at,)), (1, (at,))]

    outs = [((ys - 1, *one), [((y - 1,), pair(1, 1, y)) for y in others])]
    outs += [(one, [(whole, pair(0, 1, y))]) for y in others]
    outs += [(one, [(whole, pair(1, 1, 0))])]
    outs += [(one, [(whole, pair(0, 0, y))]) for y in others]
    diag_x, *rest = add_up(outs, [kept0, got0], name="stage1")
    after = [diag_x]
    diag_y, side_x, side_y = rest[: ys - 1], rest[ys - 1], rest[ys:]
    diag_x = x_flip(diag_x)
    diag_y = [y_flip(d, y) for y, d in zip(others, diag_y)]
    side_x = x_flip(side_x)
    side_y = [y_flip(d, y) for y, d in zip(others, side_y)]

    step = zs // 4
    while step:
        outs = [((len(places), 2, rows, half), [((i,), [place]) for i, place in enumerate(places)])]
        (to_z,) = add_up(outs, held, after, name="widen")
        after = [to_z]
        held.append(z_flip(to_z, step))
        places = places + [(len(held) - 1, (i,)) for i in range(len(places))]
        offsets = offsets + [z ^ step for z in offsets]
        step //= 2

    outs = [(one, [(whole, pair(0, 1, 0) + [(2 + y, whole) for y in others])])]
    outs += [(one, [(whole, pair(1, 0, y) + [(2, (y - 1,))])]) for y in others]
    last_x, *last_y = add_up(outs, [kept1, got1, diag_x, *diag_y], after, name="stage2")
    after = last_x
    last_x = x_flip(last_x)
    last_y = [y_flip(d, y) for y, d in zip(others, last_y)]

    sums = [
        pair(0, 0, 0) + [(2 + y, whole) for y in others],
        pair(1, 0, 0) + [(2, whole)],
    ]
    outs = [((2, *one), [((h,), sums[h]) for h in range(2)])]
    (base,) = add_up(outs, [kept1, got1, side_x, *side_y], [after], name="sides", kind=F32)

    outs = [(one, [((z,), [(a, i + (h,))]) for z, (a, i) in zip(offsets, places)]) for h in range(2)]
    own = list(add_up(outs, held, [base], name="own"))
    on_x = [x_flip(own[0])]
    on_y = [[None, y_flip(own[1], y)] for y in others]
    on_x.append(x_flip(own[1]))
    for y in others:
        on_y[y - 1][0] = y_flip(own[0], y)
    diag = [[y_flip(on_x[0], y), x_flip(on_y[y - 1][1])] for y in others]

    arrays = [base, last_x, *last_y]
    plane = [[(0, (0,)), (1, ())], [(0, (1,))] + [(1 + y, ()) for y in others]]
    left = list(range(zs))
    sums = {(z, h): [(a, i + (z,)) for a, i in plane[h]] for z in left for h in range(2)}
    after = [own[0]]
    step = 1
    while step < zs:
        going = [z for z in left if z & step]
        left = [z for z in left if not z & step]
        outs = [((len(going), 2, rows, half), [((i, h), sums[z, h]) for i, z in enumerate(going) for h in range(2)])]
        (to_z,) = add_up(outs, arrays, after, name="plane")
        arrays = [*arrays, z_flip(to_z, step)]
        after = [to_z]
        sums = {(z, h): sums[z, h] + [(len(arrays) - 1, (i, h))] for i, z in enumerate(left) for h in range(2)}
        step *= 2
    weight_grad = finish([sums[0, 0], sums[0, 1]], arrays, tokens)

    held = own + [e for es in on_y for e in es] + on_x
    places = [((i,), [(i, whole)]) for i in range(len(held))]
    (most,) = add_up([((len(held), *one), places)], held, name="most")
    held = [d for ds in diag for d in ds]
    places = [((i,), [(i, whole)]) for i in range(len(held))]
    (last,) = add_up([((len(held), *one), places)], held, [to_z], name="last")
    projected = make_project(tokens, [most, last, core_flip(most), core_flip(last)], ys, zs)
    return projected, weight_grad.T


def solution(mesh):
    placed = (
        P(("wide", "node"), None),
        P("wide", "node"),
        P(None, "node"),
        P(("wide", "node"), None),
    )
    return jax.shard_map(
        functools.partial(on_device, mesh.shape["wide"], mesh.shape["node"]),
        mesh=mesh,
        in_specs=placed,
        out_specs=(P(("wide", "node"), None), P("wide", "node")),
        check_vma=False,
    )
```

```python
import functools

import jax
import jax.numpy as jnp
from jax import lax
from jax.experimental import pallas as pl
from jax.experimental.pallas import tpu as pltpu
from jax.sharding import PartitionSpec as P

BLOCK = 128
F32 = jnp.float32
BF16 = jnp.bfloat16
NT = (((1,), (1,)), ((), ()))
VMEM = pl.BlockSpec(memory_space=pltpu.VMEM)
ANY = pl.BlockSpec(memory_space=pl.ANY)
PARAMS = pltpu.CompilerParams(vmem_limit_bytes=10 << 20)


def place_of(h, x, y, ys):
    return 2 * (ys * x + y) + h


def turn_of(h, x, y, ys):
    if x and y:
        return 0, 2 * (y - 1) + h
    if (x and h) or (y and not h):
        return 0, 2 * (ys - 1) + y
    return 1, (2 + y if x or y else h)


def flip(entries, axis, offset, size):
    return lax.ppermute(entries, axis, [(i, i ^ offset) for i in range(size)])


def columns_of(x, z, cols):
    place = lax.bitwise_xor(lax.axis_index("wide"), 2 * z + x) * cols
    return pl.ds(pl.multiple_of(place, cols), cols)


def first_kernel(ys, zs, tokens, cot, codes, scales, *refs):
    (*made, weight, tokens_v, cot_v, codes_v, scales_v, cot_t, sems) = refs
    rows, cols = codes.shape
    half = cols // 2
    fetched = []

    def fetch(src, dst):
        fetched.append(pltpu.make_async_copy(src, dst, sems.at[len(fetched)]))
        fetched[-1].start()

    for src, dst in ((cot, cot_v), (codes, codes_v), (scales, scales_v)):
        fetch(src, dst)
    order = [(x, z) for x in (1, 0) for z in range(zs)]
    for x, z in order:
        place = columns_of(x, z, cols)
        fetch(tokens.at[:, place], tokens_v.at[:, place])
    for copy in fetched[:3]:
        copy.wait()

    blocks = cols // BLOCK
    first = lax.axis_index("wide") * blocks
    shape = (scales.shape[1], blocks)
    chosen = lax.broadcasted_iota(jnp.int32, shape, 0) == first + lax.broadcasted_iota(jnp.int32, shape, 1)
    factor = jnp.dot(scales_v[...], chosen.astype(F32).astype(BF16), preferred_element_type=F32)
    for b in range(blocks):
        at = b * BLOCK
        piece = (codes_v[:, at : at + BLOCK].astype(F32) * factor[:, b : b + 1]).astype(BF16)
        weight[at // half, :, at % half : at % half + BLOCK] = piece

    cot_t[...] = cot_v[...].astype(F32).T.astype(BF16)
    node = lax.axis_index("node")
    names = [(core, y) for core in (1, 0) for y in range(ys)]
    picked = []
    for core, y in names:
        place = lax.bitwise_xor(node, 2 * y + core) * rows
        picked.append(cot_t[pl.ds(pl.multiple_of(place, rows), rows), :])
    left = jnp.concatenate(picked, axis=0)
    for copy, (x, z) in zip(fetched[3:], order):
        copy.wait()
        right = tokens_v[:, columns_of(x, z, cols)]
        for h in range(2):
            part = jnp.dot(left, right[:, h * half : (h + 1) * half], preferred_element_type=F32).astype(BF16)
            for i, (core, y) in enumerate(names):
                turn, at = turn_of(h, x, y, ys)
                made[2 * (1 - core) + turn][at, z] = part[i * rows : (i + 1) * rows]


def local_products(tokens, cot, codes, scales, ys, zs):
    rows, cols = codes.shape
    half = cols // 2
    operands = (tokens, cot, codes, scales)
    blocks = [jax.ShapeDtypeStruct((n, zs, rows, half), BF16) for n in (3 * ys - 2, ys + 2)]
    return pl.pallas_call(
        functools.partial(first_kernel, ys, zs),
        out_shape=(*blocks, *blocks, jax.ShapeDtypeStruct((2, rows, half), BF16)),
        in_specs=[ANY] * 4,
        out_specs=(VMEM,) * 5,
        scratch_shapes=[pltpu.VMEM(a.shape, BF16) for a in operands]
        + [pltpu.VMEM(cot.shape[::-1], BF16), pltpu.SemaphoreType.DMA((3 + 2 * zs,))],
        compiler_params=PARAMS,
        cost_estimate=pl.CostEstimate(
            flops=2 * tokens.size * cot.shape[1], bytes_accessed=4 * tokens.size, transcendentals=0
        ),
        name="first",
    )(*[pltpu.with_memory_space_constraint(a, pltpu.HBM) for a in operands])


def plain_products(tokens, cot, codes, scales, ys, zs):
    rows, cols = codes.shape
    half = cols // 2
    node, wide = lax.axis_index("node"), lax.axis_index("wide")
    part = jnp.dot(cot.T, tokens, preferred_element_type=F32).astype(BF16)
    part = part.reshape(2 * ys, rows, 2 * zs, 2, half).transpose(3, 0, 2, 1, 4)
    part = jnp.take(part, jnp.arange(2 * ys) ^ node, axis=1)
    part = jnp.take(part, jnp.arange(2 * zs) ^ wide, axis=2)
    part = part.reshape(2, ys, 2, zs, 2, rows, half).transpose(2, 4, 1, 0, 3, 5, 6)
    part = part.reshape(2, 4 * ys, zs, rows, half)
    split = []
    for core in (1, 0):
        named = {turn_of(h, x, y, ys): part[core, place_of(h, x, y, ys)] for h in range(2) for x in range(2) for y in range(ys)}
        for turn, count in enumerate((3 * ys - 2, ys + 2)):
            split.append(jnp.stack([named[turn, i] for i in range(count)]))
    index = (wide * cols + jnp.arange(cols)) // BLOCK
    factor = jnp.take(scales, index, axis=1).astype(F32)
    weight = (codes.astype(F32) * factor).astype(BF16)
    weight = weight.reshape(rows, 2, half).transpose(1, 0, 2)
    return *split, weight


def add_up(outs, arrays, after=(), name="add_up", kind=BF16):
    shapes = [jax.ShapeDtypeStruct(shape, kind) for shape, _ in outs]
    rows, half = arrays[0].shape[-2:]
    if half % BLOCK or rows % 16:
        results = []
        for shape, places in outs:
            result = jnp.zeros(shape, kind)
            for at, terms in places:
                total = sum(arrays[a][i].astype(F32) for a, i in terms)
                result = result.at[at].set(total.astype(kind))
            results.append(result)
        return results

    def kernel(*refs):
        given, made = refs[: len(arrays)], refs[len(arrays) + len(after) :]
        for out, (_, places) in zip(made, outs):
            for at, terms in places:
                terms = [given[a][i] for a, i in terms]
                if len(terms) > 1:
                    terms = [sum(t.astype(F32) for t in terms).astype(kind)]
                out[at] = terms[0]

    return pl.pallas_call(
        kernel,
        out_shape=shapes,
        in_specs=[VMEM] * len(arrays) + [ANY] * len(after),
        out_specs=[VMEM] * len(outs),
        compiler_params=PARAMS,
        name=name,
    )(*arrays, *after)


def finish(sums, arrays, after):
    rows, half = arrays[0].shape[-2:]

    def total(given, h):
        return sum(given[a][i].astype(F32) for a, i in sums[h])

    if half % BLOCK or rows % 16:
        return jnp.concatenate([total(arrays, h) for h in range(2)], axis=1)

    def kernel(*refs):
        for h in range(2):
            refs[-1][:, h * half : (h + 1) * half] = total(refs[:-2], h)

    return pl.pallas_call(
        kernel,
        out_shape=jax.ShapeDtypeStruct((rows, 2 * half), F32),
        in_specs=[VMEM] * len(arrays) + [ANY],
        out_specs=VMEM,
        compiler_params=PARAMS,
        cost_estimate=pl.CostEstimate(flops=4 * 10**10, bytes_accessed=1, transcendentals=0),
        name="finish",
    )(*arrays, after)


def project_kernel(ys, zs, x, tokens, *refs):
    if x == 0:
        (*weights, out) = refs
        total = 0.0
    else:
        (*weights, earlier, out, total_t) = refs
        total = earlier[...]
    count = len(weights) // 2
    rows, half = weights[0].shape[2:]
    cols = 2 * half
    for z in range(zs):
        pieces = tokens[:, columns_of(x, z, cols)]
        for h in range(2):
            picked = []
            for n in range(2 * ys):
                held = weights[count * (n % 2) : count * (n % 2 + 1)]
                y = n // 2
                if x and y:
                    picked.append(held[1 + 2 * (y - 1) + h][z])
                else:
                    picked.append(held[0][2 * y + h, z])
            left = jnp.concatenate(picked, axis=0)
            right = pieces[:, h * half : (h + 1) * half]
            total = total + lax.dot_general(left, right, NT, preferred_element_type=F32)
    if x == 0:
        out[...] = total
        return
    node = lax.axis_index("node")
    total_t[...] = total.reshape(total_t.shape)
    ordered = [total_t[lax.bitwise_xor(node, n)] for n in range(2 * ys)]
    out[...] = jnp.concatenate(ordered, axis=0).T.astype(BF16)


def project(tokens, near, far, ys, zs):
    rows = near[0].shape[2]
    count, width = tokens.shape[0], 2 * ys * rows
    cost = pl.CostEstimate(flops=tokens.size * width, bytes_accessed=2 * tokens.size, transcendentals=0)
    earlier = pl.pallas_call(
        functools.partial(project_kernel, ys, zs, 0),
        out_shape=jax.ShapeDtypeStruct((width, count), F32),
        in_specs=[VMEM] * (1 + len(near)),
        out_specs=VMEM,
        compiler_params=PARAMS,
        cost_estimate=cost,
        name="project_near",
    )(tokens, *near)
    return pl.pallas_call(
        functools.partial(project_kernel, ys, zs, 1),
        out_shape=jax.ShapeDtypeStruct((count, width), BF16),
        in_specs=[VMEM] * (2 + len(far)),
        out_specs=VMEM,
        scratch_shapes=[pltpu.VMEM((2 * ys, rows, count), F32)],
        compiler_params=PARAMS,
        cost_estimate=cost,
        name="project_far",
    )(tokens, *far, earlier)


def plain_project(tokens, near, far, ys, zs):
    rows, half = near[0].shape[2:]
    node, wide = lax.axis_index("node"), lax.axis_index("wide")
    pieces = tokens.reshape(tokens.shape[0], 2 * zs, 2, half)
    pieces = jnp.take(pieces, jnp.arange(2 * zs) ^ wide, axis=1)
    pieces = pieces.reshape(tokens.shape[0], zs, 2, 2, half)
    count = len(far) // 2
    weights = [
        jnp.concatenate([near[c], far[count * c], jnp.stack(far[count * c + 1 : count * (c + 1)])]) for c in range(2)
    ]
    total = []
    for n in range(2 * ys):
        part = 0.0
        for h in range(2):
            for x in range(2):
                held = weights[n % 2][place_of(h, x, n // 2, ys)]
                part = part + jnp.einsum("tzl,zrl->tr", pieces[:, :, x, h], held, preferred_element_type=F32)
        total.append(part)
    total = jnp.take(jnp.stack(total, axis=1), jnp.arange(2 * ys) ^ node, axis=1)
    return total.reshape(tokens.shape[0], -1).astype(BF16)


def on_device(wides, nodes, tokens, codes, scales, cotangent):
    ys, zs = nodes // 2, wides // 2
    cols, rows = codes.shape
    half = cols // 2
    aligned = half % BLOCK == 0 and rows % 16 == 0
    products, make_project = (local_products, project) if aligned else (plain_products, plain_project)
    others = range(1, ys)
    one = (zs, rows, half)
    whole = (...,)

    def core_flip(entries):
        return flip(entries, "node", 1, nodes)

    def y_flip(entries, y):
        return flip(entries, "node", 2 * y, nodes)

    def x_flip(entries):
        return flip(entries, "wide", 1, wides)

    def z_flip(entries, z):
        return flip(entries, "wide", 2 * z, wides)

    sent0, sent1, kept0, kept1, weight = products(tokens, cotangent, codes.T, scales.T, ys, zs)

    got0, got1 = core_flip(sent0), core_flip(sent1)
    held = [weight, z_flip(weight, zs // 2)]
    offsets = [0, zs // 2]
    places = [(0, ()), (1, ())]

    def pair(h, x, y):
        _, at = turn_of(h, x, y, ys)
        return [(0, (at,)), (1, (at,))]

    outs = [((ys - 1, *one), [((y - 1,), pair(1, 1, y)) for y in others])]
    outs += [(one, [(whole, pair(0, 1, y))]) for y in others]
    outs += [(one, [(whole, pair(1, 1, 0))])]
    outs += [(one, [(whole, pair(0, 0, y))]) for y in others]
    diag_x, *rest = add_up(outs, [kept0, got0], name="stage1")
    after = [diag_x]
    diag_y, side_x, side_y = rest[: ys - 1], rest[ys - 1], rest[ys:]
    diag_x = x_flip(diag_x)
    diag_y = [y_flip(d, y) for y, d in zip(others, diag_y)]
    side_x = x_flip(side_x)
    side_y = [y_flip(d, y) for y, d in zip(others, side_y)]

    step = zs // 4
    while step:
        outs = [((len(places), 2, rows, half), [((i,), [place]) for i, place in enumerate(places)])]
        (to_z,) = add_up(outs, held, after, name="widen")
        after = [to_z]
        held.append(z_flip(to_z, step))
        places = places + [(len(held) - 1, (i,)) for i in range(len(places))]
        offsets = offsets + [z ^ step for z in offsets]
        step //= 2

    outs = [(one, [(whole, pair(0, 1, 0) + [(2 + y, whole) for y in others])])]
    outs += [(one, [(whole, pair(1, 0, y) + [(2, (y - 1,))])]) for y in others]
    last_x, *last_y = add_up(outs, [kept1, got1, diag_x, *diag_y], after, name="stage2")
    after = last_x
    last_x = x_flip(last_x)
    last_y = [y_flip(d, y) for y, d in zip(others, last_y)]

    sums = [
        pair(0, 0, 0) + [(2 + y, whole) for y in others],
        pair(1, 0, 0) + [(2, whole)],
    ]
    outs = [((2, *one), [((h,), sums[h]) for h in range(2)])]
    (base,) = add_up(outs, [kept1, got1, side_x, *side_y], [after], name="sides", kind=F32)

    outs = [(one, [((z,), [(a, i + (h,))]) for z, (a, i) in zip(offsets, places)]) for h in range(2)]
    own = list(add_up(outs, held, [base], name="own"))
    on_x = [x_flip(own[0])]
    on_y = [[None, y_flip(own[1], y)] for y in others]
    on_x.append(x_flip(own[1]))
    for y in others:
        on_y[y - 1][0] = y_flip(own[0], y)
    diag = [[y_flip(on_x[0], y), x_flip(on_y[y - 1][1])] for y in others]

    arrays = [base, last_x, *last_y]
    plane = [[(0, (0,)), (1, ())], [(0, (1,))] + [(1 + y, ()) for y in others]]
    left = list(range(zs))
    sums = {(z, h): [(a, i + (z,)) for a, i in plane[h]] for z in left for h in range(2)}
    after = [own[0]]
    step = 1
    while step < zs:
        going = [z for z in left if z & step]
        left = [z for z in left if not z & step]
        outs = [((len(going), 2, rows, half), [((i, h), sums[z, h]) for i, z in enumerate(going) for h in range(2)])]
        (to_z,) = add_up(outs, arrays, after, name="plane")
        arrays = [*arrays, z_flip(to_z, step)]
        after = [to_z]
        sums = {(z, h): sums[z, h] + [(len(arrays) - 1, (i, h))] for i, z in enumerate(left) for h in range(2)}
        step *= 2
    weight_grad = finish([sums[0, 0], sums[0, 1]], arrays, tokens)

    held = own + [e for es in on_y for e in es] + on_x
    groups = [range(2 * ys), range(2 * ys, 2 * ys + 2)]
    outs = [((len(g), *one), [((i - g[0],), [(i, whole)]) for i in g]) for g in groups]
    near, side = add_up(outs, held, name="most")
    ends = [d for ds in diag for d in ds]
    near = [near, core_flip(near)]
    far = [side, *ends, core_flip(side), *[core_flip(e) for e in ends]]
    projected = make_project(tokens, near, far, ys, zs)
    return projected, weight_grad.T


def solution(mesh):
    placed = (
        P(("wide", "node"), None),
        P("wide", "node"),
        P(None, "node"),
        P(("wide", "node"), None),
    )
    return jax.shard_map(
        functools.partial(on_device, mesh.shape["wide"], mesh.shape["node"]),
        mesh=mesh,
        in_specs=placed,
        out_specs=(P(("wide", "node"), None), P("wide", "node")),
        check_vma=False,
    )
```

```python
import functools

import jax
import jax.numpy as jnp
from jax import lax
from jax.experimental import pallas as pl
from jax.experimental.pallas import tpu as pltpu
from jax.sharding import PartitionSpec as P

BLOCK = 128
F32 = jnp.float32
BF16 = jnp.bfloat16
NT = (((1,), (1,)), ((), ()))
VMEM = pl.BlockSpec(memory_space=pltpu.VMEM)
ANY = pl.BlockSpec(memory_space=pl.ANY)
PARAMS = pltpu.CompilerParams(vmem_limit_bytes=10 << 20)


def place_of(h, x, y, ys):
    return 2 * (ys * x + y) + h


def turn_of(h, x, y, ys):
    if x and y:
        return 0, 2 * (y - 1) + h
    if (x and h) or (y and not h):
        return 0, 2 * (ys - 1) + y
    return 1, (2 + y if x or y else h)


def flip(entries, axis, offset, size):
    return lax.ppermute(entries, axis, [(i, i ^ offset) for i in range(size)])


def columns_of(x, z, cols):
    place = lax.bitwise_xor(lax.axis_index("wide"), 2 * z + x) * cols
    return pl.ds(pl.multiple_of(place, cols), cols)


def store_products(left, tokens, x, z, ys, made):
    refs = list(made.values())
    rows, half = refs[0].shape[2:]
    right = tokens[:, columns_of(x, z, 2 * half)]
    for h in range(2):
        names = [(c, y) for c in (1, 0) for y in range(ys) if (c, turn_of(h, x, y, ys)[0]) in made]
        if not names:
            continue
        picked = [left[((1 - c) * ys + y) * rows :][:rows] for c, y in names]
        picked = picked[0] if len(picked) == 1 else jnp.concatenate(picked, axis=0)
        part = jnp.dot(picked, right[:, h * half : (h + 1) * half], preferred_element_type=F32).astype(BF16)
        for i, (c, y) in enumerate(names):
            turn, at = turn_of(h, x, y, ys)
            made[c, turn][at, z] = part[i * rows : (i + 1) * rows]


def first_kernel(ys, zs, tokens, cot, sent0, left, held, cot_v, cot_t, sems):
    cols = tokens.shape[1] // (2 * zs)
    rows = sent0.shape[2]
    small = pltpu.make_async_copy(cot, cot_v, sems.at[0])
    small.start()
    order = [(x, z) for x in (1, 0) for z in range(zs)]
    copies = []
    for i, (x, z) in enumerate(order):
        place = columns_of(x, z, cols)
        copies.append(pltpu.make_async_copy(tokens.at[:, place], held.at[:, place], sems.at[1 + i]))
        copies[-1].start()
    small.wait()
    cot_t[...] = cot_v[...].astype(F32).T.astype(BF16)
    node = lax.axis_index("node")
    picked = []
    for core in (1, 0):
        for y in range(ys):
            place = lax.bitwise_xor(node, 2 * y + core) * rows
            picked.append(cot_t[pl.ds(pl.multiple_of(place, rows), rows), :])
    ordered = jnp.concatenate(picked, axis=0)
    left[...] = ordered
    for copy, (x, z) in zip(copies, order):
        copy.wait()
        store_products(ordered, held, x, z, ys, {(1, 0): sent0})


def second_kernel(ys, zs, held, left, codes, scales, sent1, kept0, kept1, weight):
    cols = codes.shape[1]
    half = cols // 2
    blocks = cols // BLOCK
    first = lax.axis_index("wide") * blocks
    shape = (scales.shape[1], blocks)
    chosen = lax.broadcasted_iota(jnp.int32, shape, 0) == first + lax.broadcasted_iota(jnp.int32, shape, 1)
    factor = jnp.dot(scales[...], chosen.astype(F32).astype(BF16), preferred_element_type=F32)
    for b in range(blocks):
        at = b * BLOCK
        piece = codes[:, at : at + BLOCK].astype(F32) * factor[:, b : b + 1]
        weight[at // half, :, at % half : at % half + BLOCK] = piece.astype(BF16)
    ordered = left[...]
    for x in (1, 0):
        for z in range(zs):
            store_products(ordered, held, x, z, ys, {(1, 1): sent1, (0, 0): kept0, (0, 1): kept1})


def local_products(tokens, cot, codes, scales, ys, zs):
    rows, cols = codes.shape
    half = cols // 2
    blocks = [jax.ShapeDtypeStruct((n, zs, rows, half), BF16) for n in (3 * ys - 2, ys + 2)]
    turned = jax.ShapeDtypeStruct(cot.shape[::-1], BF16)
    cost = pl.CostEstimate(flops=tokens.size * cot.shape[1], bytes_accessed=3 * tokens.size, transcendentals=0)
    sent0, left, held = pl.pallas_call(
        functools.partial(first_kernel, ys, zs),
        out_shape=(blocks[0], turned, jax.ShapeDtypeStruct(tokens.shape, BF16)),
        in_specs=[ANY] * 2,
        out_specs=(VMEM,) * 3,
        scratch_shapes=[
            pltpu.VMEM(cot.shape, BF16),
            pltpu.VMEM(turned.shape, BF16),
            pltpu.SemaphoreType.DMA((1 + 2 * zs,)),
        ],
        compiler_params=PARAMS,
        cost_estimate=cost,
        name="first",
    )(*[pltpu.with_memory_space_constraint(a, pltpu.HBM) for a in (tokens, cot)])
    sent1, kept0, kept1, weight = pl.pallas_call(
        functools.partial(second_kernel, ys, zs),
        out_shape=(blocks[1], *blocks, jax.ShapeDtypeStruct((2, rows, half), BF16)),
        in_specs=[VMEM] * 4,
        out_specs=(VMEM,) * 4,
        compiler_params=PARAMS,
        cost_estimate=cost,
        name="second",
    )(held, left, codes, scales)
    return sent0, sent1, kept0, kept1, weight


def plain_products(tokens, cot, codes, scales, ys, zs):
    rows, cols = codes.shape
    half = cols // 2
    node, wide = lax.axis_index("node"), lax.axis_index("wide")
    part = jnp.dot(cot.T, tokens, preferred_element_type=F32).astype(BF16)
    part = part.reshape(2 * ys, rows, 2 * zs, 2, half).transpose(3, 0, 2, 1, 4)
    part = jnp.take(part, jnp.arange(2 * ys) ^ node, axis=1)
    part = jnp.take(part, jnp.arange(2 * zs) ^ wide, axis=2)
    part = part.reshape(2, ys, 2, zs, 2, rows, half).transpose(2, 4, 1, 0, 3, 5, 6)
    part = part.reshape(2, 4 * ys, zs, rows, half)
    split = []
    for core in (1, 0):
        named = {turn_of(h, x, y, ys): part[core, place_of(h, x, y, ys)] for h in range(2) for x in range(2) for y in range(ys)}
        for turn, count in enumerate((3 * ys - 2, ys + 2)):
            split.append(jnp.stack([named[turn, i] for i in range(count)]))
    index = (wide * cols + jnp.arange(cols)) // BLOCK
    factor = jnp.take(scales, index, axis=1).astype(F32)
    weight = (codes.astype(F32) * factor).astype(BF16)
    weight = weight.reshape(rows, 2, half).transpose(1, 0, 2)
    return *split, weight


def add_up(outs, arrays, after=(), name="add_up", kind=BF16):
    shapes = [jax.ShapeDtypeStruct(shape, kind) for shape, _ in outs]
    rows, half = arrays[0].shape[-2:]
    if half % BLOCK or rows % 16:
        results = []
        for shape, places in outs:
            result = jnp.zeros(shape, kind)
            for at, terms in places:
                total = sum(arrays[a][i].astype(F32) for a, i in terms)
                result = result.at[at].set(total.astype(kind))
            results.append(result)
        return results

    def kernel(*refs):
        given, made = refs[: len(arrays)], refs[len(arrays) + len(after) :]
        for out, (_, places) in zip(made, outs):
            for at, terms in places:
                terms = [given[a][i] for a, i in terms]
                if len(terms) > 1:
                    terms = [sum(t.astype(F32) for t in terms).astype(kind)]
                out[at] = terms[0]

    return pl.pallas_call(
        kernel,
        out_shape=shapes,
        in_specs=[VMEM] * len(arrays) + [ANY] * len(after),
        out_specs=[VMEM] * len(outs),
        compiler_params=PARAMS,
        name=name,
    )(*arrays, *after)


def finish(sums, arrays, after):
    rows, half = arrays[0].shape[-2:]

    def total(given, h):
        return sum(given[a][i].astype(F32) for a, i in sums[h])

    if half % BLOCK or rows % 16:
        return jnp.concatenate([total(arrays, h) for h in range(2)], axis=1)

    def kernel(*refs):
        for h in range(2):
            refs[-1][:, h * half : (h + 1) * half] = total(refs[:-2], h)

    return pl.pallas_call(
        kernel,
        out_shape=jax.ShapeDtypeStruct((rows, 2 * half), F32),
        in_specs=[VMEM] * len(arrays) + [ANY],
        out_specs=VMEM,
        compiler_params=PARAMS,
        cost_estimate=pl.CostEstimate(flops=4 * 10**10, bytes_accessed=1, transcendentals=0),
        name="finish",
    )(*arrays, after)


def project_kernel(ys, zs, x, tokens, *refs):
    if x == 0:
        (*weights, out) = refs
        total = 0.0
    else:
        (earlier, *weights, out, total_t) = refs
        total = earlier[...]
    count = len(weights) // 2
    rows, half = weights[0].shape[2:]
    cols = 2 * half
    for z in range(zs):
        pieces = tokens[:, columns_of(x, z, cols)]
        for h in range(2):
            picked = []
            for n in range(2 * ys):
                held = weights[count * (n % 2) : count * (n % 2 + 1)]
                y = n // 2
                if x and y:
                    picked.append(held[1 + 2 * (y - 1) + h][z])
                else:
                    picked.append(held[0][2 * y + h, z])
            left = jnp.concatenate(picked, axis=0)
            right = pieces[:, h * half : (h + 1) * half]
            total = total + lax.dot_general(left, right, NT, preferred_element_type=F32)
    if x == 0:
        out[...] = total
        return
    node = lax.axis_index("node")
    total_t[...] = total.reshape(total_t.shape)
    ordered = [total_t[lax.bitwise_xor(node, n)] for n in range(2 * ys)]
    out[...] = jnp.concatenate(ordered, axis=0).T.astype(BF16)


def project(tokens, near, far, ys, zs):
    rows = near[0].shape[2]
    count, width = tokens.shape[0], 2 * ys * rows
    cost = pl.CostEstimate(flops=tokens.size * width, bytes_accessed=2 * tokens.size, transcendentals=0)
    earlier = pl.pallas_call(
        functools.partial(project_kernel, ys, zs, 0),
        out_shape=jax.ShapeDtypeStruct((width, count), F32),
        in_specs=[VMEM] * (1 + len(near)),
        out_specs=VMEM,
        compiler_params=PARAMS,
        cost_estimate=cost,
        name="project_near",
    )(tokens, *near)
    return pl.pallas_call(
        functools.partial(project_kernel, ys, zs, 1),
        out_shape=jax.ShapeDtypeStruct((count, width), BF16),
        in_specs=[VMEM] * (2 + len(far)),
        out_specs=VMEM,
        scratch_shapes=[pltpu.VMEM((2 * ys, rows, count), F32)],
        compiler_params=PARAMS,
        cost_estimate=cost,
        name="project_far",
    )(tokens, earlier, *far)


def plain_project(tokens, near, far, ys, zs):
    rows, half = near[0].shape[2:]
    node, wide = lax.axis_index("node"), lax.axis_index("wide")
    pieces = tokens.reshape(tokens.shape[0], 2 * zs, 2, half)
    pieces = jnp.take(pieces, jnp.arange(2 * zs) ^ wide, axis=1)
    pieces = pieces.reshape(tokens.shape[0], zs, 2, 2, half)
    count = len(far) // 2
    weights = [
        jnp.concatenate([near[c], far[count * c], jnp.stack(far[count * c + 1 : count * (c + 1)])]) for c in range(2)
    ]
    total = []
    for n in range(2 * ys):
        part = 0.0
        for h in range(2):
            for x in range(2):
                held = weights[n % 2][place_of(h, x, n // 2, ys)]
                part = part + jnp.einsum("tzl,zrl->tr", pieces[:, :, x, h], held, preferred_element_type=F32)
        total.append(part)
    total = jnp.take(jnp.stack(total, axis=1), jnp.arange(2 * ys) ^ node, axis=1)
    return total.reshape(tokens.shape[0], -1).astype(BF16)


def on_device(wides, nodes, tokens, codes, scales, cotangent):
    ys, zs = nodes // 2, wides // 2
    cols, rows = codes.shape
    half = cols // 2
    aligned = half % BLOCK == 0 and rows % 16 == 0
    products, make_project = (local_products, project) if aligned else (plain_products, plain_project)
    others = range(1, ys)
    one = (zs, rows, half)
    whole = (...,)

    def core_flip(entries):
        return flip(entries, "node", 1, nodes)

    def y_flip(entries, y):
        return flip(entries, "node", 2 * y, nodes)

    def x_flip(entries):
        return flip(entries, "wide", 1, wides)

    def z_flip(entries, z):
        return flip(entries, "wide", 2 * z, wides)

    sent0, sent1, kept0, kept1, weight = products(tokens, cotangent, codes.T, scales.T, ys, zs)

    got0, got1 = core_flip(sent0), core_flip(sent1)
    held = [weight, z_flip(weight, zs // 2)]
    offsets = [0, zs // 2]
    places = [(0, ()), (1, ())]

    def pair(h, x, y):
        _, at = turn_of(h, x, y, ys)
        return [(0, (at,)), (1, (at,))]

    outs = [((ys - 1, *one), [((y - 1,), pair(1, 1, y)) for y in others])]
    outs += [(one, [(whole, pair(0, 1, y))]) for y in others]
    outs += [(one, [(whole, pair(0, 0, y))]) for y in others]
    outs += [(one, [(whole, pair(1, 1, 0))])]
    diag_x, *rest = add_up(outs, [kept0, got0], name="stage1")
    after = [diag_x]
    diag_y, side_y, side_x = rest[: ys - 1], rest[ys - 1 : -1], rest[-1]
    diag_x = x_flip(diag_x)
    diag_y = [y_flip(d, y) for y, d in zip(others, diag_y)]
    side_y = [y_flip(d, y) for y, d in zip(others, side_y)]
    side_x = x_flip(side_x)

    step = zs // 4
    while step:
        outs = [((len(places), 2, rows, half), [((i,), [place]) for i, place in enumerate(places)])]
        (to_z,) = add_up(outs, held, after, name="widen")
        after = [to_z]
        held.append(z_flip(to_z, step))
        places = places + [(len(held) - 1, (i,)) for i in range(len(places))]
        offsets = offsets + [z ^ step for z in offsets]
        step //= 2

    outs = [(one, [(whole, pair(0, 1, 0) + [(2 + y, whole) for y in others])])]
    outs += [(one, [(whole, pair(1, 0, y) + [(2, (y - 1,))])]) for y in others]
    last_x, *last_y = add_up(outs, [kept1, got1, diag_x, *diag_y], after, name="stage2")
    after = last_x
    last_x = x_flip(last_x)
    last_y = [y_flip(d, y) for y, d in zip(others, last_y)]

    sums = [
        pair(0, 0, 0) + [(1 + y, whole) for y in others],
        pair(1, 0, 0) + [(1 + ys, whole)],
    ]
    outs = [((2, *one), [((h,), sums[h]) for h in range(2)])]
    (base,) = add_up(outs, [kept1, got1, *side_y, side_x], [after], name="sides", kind=F32)

    outs = [(one, [((z,), [(a, i + (h,))]) for z, (a, i) in zip(offsets, places)]) for h in range(2)]
    own = list(add_up(outs, held, [base], name="own"))
    on_x = [x_flip(own[0])]
    on_y = [[None, y_flip(own[1], y)] for y in others]
    on_x.append(x_flip(own[1]))
    for y in others:
        on_y[y - 1][0] = y_flip(own[0], y)
    diag = [[y_flip(on_x[0], y), x_flip(on_y[y - 1][1])] for y in others]

    arrays = [base, last_x, *last_y]
    plane = [[(0, (0,)), (1, ())], [(0, (1,))] + [(1 + y, ()) for y in others]]
    left = list(range(zs))
    sums = {(z, h): [(a, i + (z,)) for a, i in plane[h]] for z in left for h in range(2)}
    after = [own[0]]
    step = 1
    while step < zs:
        going = [z for z in left if z & step]
        left = [z for z in left if not z & step]
        outs = [((len(going), 2, rows, half), [((i, h), sums[z, h]) for i, z in enumerate(going) for h in range(2)])]
        (to_z,) = add_up(outs, arrays, after, name="plane")
        arrays = [*arrays, z_flip(to_z, step)]
        after = [to_z]
        sums = {(z, h): sums[z, h] + [(len(arrays) - 1, (i, h))] for i, z in enumerate(left) for h in range(2)}
        step *= 2
    weight_grad = finish([sums[0, 0], sums[0, 1]], arrays, tokens)

    held = own + [e for es in on_y for e in es]
    (near,) = add_up([((2 * ys, *one), [((i,), [(i, whole)]) for i in range(2 * ys)])], held, name="near")
    (side,) = add_up([((2, *one), [((h,), [(h, whole)]) for h in range(2)])], on_x, [near], name="side")
    ends = [d for ds in diag for d in ds]
    near = [near, core_flip(near)]
    far = [side, *ends, core_flip(side), *[core_flip(e) for e in ends]]
    projected = make_project(tokens, near, far, ys, zs)
    return projected, weight_grad.T


def solution(mesh):
    placed = (
        P(("wide", "node"), None),
        P("wide", "node"),
        P(None, "node"),
        P(("wide", "node"), None),
    )
    return jax.shard_map(
        functools.partial(on_device, mesh.shape["wide"], mesh.shape["node"]),
        mesh=mesh,
        in_specs=placed,
        out_specs=(P(("wide", "node"), None), P("wide", "node")),
        check_vma=False,
    )
```

```python
import functools

import jax
import jax.numpy as jnp
from jax import lax
from jax.experimental import pallas as pl
from jax.experimental.pallas import tpu as pltpu
from jax.sharding import PartitionSpec as P

BLOCK = 128
F32 = jnp.float32
BF16 = jnp.bfloat16
NT = (((1,), (1,)), ((), ()))
VMEM = pl.BlockSpec(memory_space=pltpu.VMEM)
ANY = pl.BlockSpec(memory_space=pl.ANY)
PARAMS = pltpu.CompilerParams(vmem_limit_bytes=10 << 20)


def place_of(h, x, y, ys):
    return 2 * (ys * x + y) + h


def turn_of(h, x, y, ys):
    if x and y:
        return 0, 2 * (y - 1) + h
    if (x and h) or (y and not h):
        return 0, 2 * (ys - 1) + y
    return 1, (2 + y if x or y else h)


def flip(entries, axis, offset, size):
    return lax.ppermute(entries, axis, [(i, i ^ offset) for i in range(size)])


def columns_of(x, z, cols):
    place = lax.bitwise_xor(lax.axis_index("wide"), 2 * z + x) * cols
    return pl.ds(pl.multiple_of(place, cols), cols)


def first_kernel(ys, zs, tokens, cot, codes, scales, *refs):
    (*made, weight, tokens_v, cot_v, codes_v, scales_v, cot_t, sems) = refs
    rows, cols = codes.shape
    half = cols // 2
    fetched = []

    def fetch(src, dst):
        fetched.append(pltpu.make_async_copy(src, dst, sems.at[len(fetched)]))
        fetched[-1].start()

    for src, dst in ((cot, cot_v), (codes, codes_v), (scales, scales_v)):
        fetch(src, dst)
    order = [(x, z) for x in (1, 0) for z in range(zs)]
    for x, z in order:
        place = columns_of(x, z, cols)
        fetch(tokens.at[:, place], tokens_v.at[:, place])
    for copy in fetched[:3]:
        copy.wait()

    blocks = cols // BLOCK
    first = lax.axis_index("wide") * blocks
    shape = (scales.shape[1], blocks)
    chosen = lax.broadcasted_iota(jnp.int32, shape, 0) == first + lax.broadcasted_iota(jnp.int32, shape, 1)
    factor = jnp.dot(scales_v[...], chosen.astype(F32).astype(BF16), preferred_element_type=F32)
    for b in range(blocks):
        at = b * BLOCK
        piece = (codes_v[:, at : at + BLOCK].astype(F32) * factor[:, b : b + 1]).astype(BF16)
        weight[at // half, :, at % half : at % half + BLOCK] = piece

    cot_t[...] = cot_v[...].astype(F32).T.astype(BF16)
    node = lax.axis_index("node")
    names = [(core, y) for core in (1, 0) for y in range(ys)]
    picked = []
    for core, y in names:
        place = lax.bitwise_xor(node, 2 * y + core) * rows
        picked.append(cot_t[pl.ds(pl.multiple_of(place, rows), rows), :])
    left = jnp.concatenate(picked, axis=0)
    for copy, (x, z) in zip(fetched[3:], order):
        copy.wait()
        right = tokens_v[:, columns_of(x, z, cols)]
        for h in range(2):
            part = jnp.dot(left, right[:, h * half : (h + 1) * half], preferred_element_type=F32).astype(BF16)
            for i, (core, y) in enumerate(names):
                turn, at = turn_of(h, x, y, ys)
                made[2 * (1 - core) + turn][at, z] = part[i * rows : (i + 1) * rows]


def local_products(tokens, cot, codes, scales, ys, zs):
    rows, cols = codes.shape
    half = cols // 2
    operands = (tokens, cot, codes, scales)
    blocks = [jax.ShapeDtypeStruct((n, zs, rows, half), BF16) for n in (3 * ys - 2, ys + 2)]
    return pl.pallas_call(
        functools.partial(first_kernel, ys, zs),
        out_shape=(*blocks, *blocks, jax.ShapeDtypeStruct((2, rows, half), BF16)),
        in_specs=[ANY] * 4,
        out_specs=(VMEM,) * 5,
        scratch_shapes=[pltpu.VMEM(a.shape, BF16) for a in operands]
        + [pltpu.VMEM(cot.shape[::-1], BF16), pltpu.SemaphoreType.DMA((3 + 2 * zs,))],
        compiler_params=PARAMS,
        cost_estimate=pl.CostEstimate(
            flops=2 * tokens.size * cot.shape[1], bytes_accessed=4 * tokens.size, transcendentals=0
        ),
        name="first",
    )(*[pltpu.with_memory_space_constraint(a, pltpu.HBM) for a in operands])


def plain_products(tokens, cot, codes, scales, ys, zs):
    rows, cols = codes.shape
    half = cols // 2
    node, wide = lax.axis_index("node"), lax.axis_index("wide")
    part = jnp.dot(cot.T, tokens, preferred_element_type=F32).astype(BF16)
    part = part.reshape(2 * ys, rows, 2 * zs, 2, half).transpose(3, 0, 2, 1, 4)
    part = jnp.take(part, jnp.arange(2 * ys) ^ node, axis=1)
    part = jnp.take(part, jnp.arange(2 * zs) ^ wide, axis=2)
    part = part.reshape(2, ys, 2, zs, 2, rows, half).transpose(2, 4, 1, 0, 3, 5, 6)
    part = part.reshape(2, 4 * ys, zs, rows, half)
    split = []
    for core in (1, 0):
        named = {turn_of(h, x, y, ys): part[core, place_of(h, x, y, ys)] for h in range(2) for x in range(2) for y in range(ys)}
        for turn, count in enumerate((3 * ys - 2, ys + 2)):
            split.append(jnp.stack([named[turn, i] for i in range(count)]))
    index = (wide * cols + jnp.arange(cols)) // BLOCK
    factor = jnp.take(scales, index, axis=1).astype(F32)
    weight = (codes.astype(F32) * factor).astype(BF16)
    weight = weight.reshape(rows, 2, half).transpose(1, 0, 2)
    return *split, weight


def add_up(outs, arrays, after=(), name="add_up", kind=BF16):
    shapes = [jax.ShapeDtypeStruct(shape, kind) for shape, _ in outs]
    rows, half = arrays[0].shape[-2:]
    if half % BLOCK or rows % 16:
        results = []
        for shape, places in outs:
            result = jnp.zeros(shape, kind)
            for at, terms in places:
                total = sum(arrays[a][i].astype(F32) for a, i in terms)
                result = result.at[at].set(total.astype(kind))
            results.append(result)
        return results

    def kernel(*refs):
        given, made = refs[: len(arrays)], refs[len(arrays) + len(after) :]
        for out, (_, places) in zip(made, outs):
            for at, terms in places:
                terms = [given[a][i] for a, i in terms]
                if len(terms) > 1:
                    terms = [sum(t.astype(F32) for t in terms).astype(kind)]
                out[at] = terms[0]

    return pl.pallas_call(
        kernel,
        out_shape=shapes,
        in_specs=[VMEM] * len(arrays) + [ANY] * len(after),
        out_specs=[VMEM] * len(outs),
        compiler_params=PARAMS,
        name=name,
    )(*arrays, *after)


def finish(sums, arrays, after):
    rows, half = arrays[0].shape[-2:]

    def total(given, h):
        return sum(given[a][i].astype(F32) for a, i in sums[h])

    if half % BLOCK or rows % 16:
        return jnp.concatenate([total(arrays, h) for h in range(2)], axis=1)

    def kernel(*refs):
        for h in range(2):
            refs[-1][:, h * half : (h + 1) * half] = total(refs[:-2], h)

    return pl.pallas_call(
        kernel,
        out_shape=jax.ShapeDtypeStruct((rows, 2 * half), F32),
        in_specs=[VMEM] * len(arrays) + [ANY],
        out_specs=VMEM,
        compiler_params=PARAMS,
        cost_estimate=pl.CostEstimate(flops=4 * 10**10, bytes_accessed=1, transcendentals=0),
        name="finish",
    )(*arrays, after)


def project_kernel(ys, zs, x, tokens, *refs):
    if x == 0:
        (*weights, out) = refs
        total = 0.0
    else:
        (*weights, earlier, out) = refs
        total = earlier[...]
    count = len(weights) // 2
    rows, half = weights[0].shape[2:]
    cols = 2 * half
    for z in range(zs):
        pieces = tokens[:, columns_of(x, z, cols)]
        for h in range(2):
            picked = []
            for n in range(2 * ys):
                held = weights[count * (n % 2) : count * (n % 2 + 1)]
                y = n // 2
                if x and y:
                    picked.append(held[1 + 2 * (y - 1) + h][z])
                else:
                    picked.append(held[0][2 * y + h, z])
            left = pieces[:, h * half : (h + 1) * half]
            right = jnp.concatenate(picked, axis=0)
            total = total + lax.dot_general(left, right, NT, preferred_element_type=F32)
    if x == 0:
        out[...] = total
        return
    node = lax.axis_index("node")
    width = total.shape[1]
    lane = lax.broadcasted_iota(jnp.int32, total.shape, 1)
    bit = 1
    while bit < 2 * ys:
        shift = bit * rows
        above = pltpu.roll(total, width - shift, 1)
        below = pltpu.roll(total, shift, 1)
        other = jnp.where(lax.bitwise_and(lane, shift) == 0, above, below)
        total = jnp.where(lax.bitwise_and(node, bit) == 0, total, other)
        bit *= 2
    out[...] = total.astype(BF16)


def project(tokens, near, far, ys, zs):
    rows = near[0].shape[2]
    count, width = tokens.shape[0], 2 * ys * rows
    cost = pl.CostEstimate(flops=tokens.size * width, bytes_accessed=2 * tokens.size, transcendentals=0)
    earlier = pl.pallas_call(
        functools.partial(project_kernel, ys, zs, 0),
        out_shape=jax.ShapeDtypeStruct((count, width), F32),
        in_specs=[VMEM] * (1 + len(near)),
        out_specs=VMEM,
        compiler_params=PARAMS,
        cost_estimate=cost,
        name="project_near",
    )(tokens, *near)
    return pl.pallas_call(
        functools.partial(project_kernel, ys, zs, 1),
        out_shape=jax.ShapeDtypeStruct((count, width), BF16),
        in_specs=[VMEM] * (2 + len(far)),
        out_specs=VMEM,
        compiler_params=PARAMS,
        cost_estimate=cost,
        name="project_far",
    )(tokens, *far, earlier)


def plain_project(tokens, near, far, ys, zs):
    rows, half = near[0].shape[2:]
    node, wide = lax.axis_index("node"), lax.axis_index("wide")
    pieces = tokens.reshape(tokens.shape[0], 2 * zs, 2, half)
    pieces = jnp.take(pieces, jnp.arange(2 * zs) ^ wide, axis=1)
    pieces = pieces.reshape(tokens.shape[0], zs, 2, 2, half)
    count = len(far) // 2
    weights = [
        jnp.concatenate([near[c], far[count * c], jnp.stack(far[count * c + 1 : count * (c + 1)])]) for c in range(2)
    ]
    total = []
    for n in range(2 * ys):
        part = 0.0
        for h in range(2):
            for x in range(2):
                held = weights[n % 2][place_of(h, x, n // 2, ys)]
                part = part + jnp.einsum("tzl,zrl->tr", pieces[:, :, x, h], held, preferred_element_type=F32)
        total.append(part)
    total = jnp.take(jnp.stack(total, axis=1), jnp.arange(2 * ys) ^ node, axis=1)
    return total.reshape(tokens.shape[0], -1).astype(BF16)


def on_device(wides, nodes, tokens, codes, scales, cotangent):
    ys, zs = nodes // 2, wides // 2
    cols, rows = codes.shape
    half = cols // 2
    aligned = half % BLOCK == 0 and rows % 16 == 0
    products, make_project = (local_products, project) if aligned else (plain_products, plain_project)
    others = range(1, ys)
    one = (zs, rows, half)
    whole = (...,)

    def core_flip(entries):
        return flip(entries, "node", 1, nodes)

    def y_flip(entries, y):
        return flip(entries, "node", 2 * y, nodes)

    def x_flip(entries):
        return flip(entries, "wide", 1, wides)

    def z_flip(entries, z):
        return flip(entries, "wide", 2 * z, wides)

    sent0, sent1, kept0, kept1, weight = products(tokens, cotangent, codes.T, scales.T, ys, zs)

    got0, got1 = core_flip(sent0), core_flip(sent1)
    held = [weight, z_flip(weight, zs // 2)]
    offsets = [0, zs // 2]
    places = [(0, ()), (1, ())]

    def pair(h, x, y):
        _, at = turn_of(h, x, y, ys)
        return [(0, (at,)), (1, (at,))]

    outs = [((ys - 1, *one), [((y - 1,), pair(1, 1, y)) for y in others])]
    outs += [(one, [(whole, pair(0, 1, y))]) for y in others]
    outs += [(one, [(whole, pair(1, 1, 0))])]
    outs += [(one, [(whole, pair(0, 0, y))]) for y in others]
    diag_x, *rest = add_up(outs, [kept0, got0], name="stage1")
    after = [diag_x]
    diag_y, side_x, side_y = rest[: ys - 1], rest[ys - 1], rest[ys:]
    diag_x = x_flip(diag_x)
    diag_y = [y_flip(d, y) for y, d in zip(others, diag_y)]
    side_x = x_flip(side_x)
    side_y = [y_flip(d, y) for y, d in zip(others, side_y)]

    step = zs // 4
    while step:
        outs = [((len(places), 2, rows, half), [((i,), [place]) for i, place in enumerate(places)])]
        (to_z,) = add_up(outs, held, after, name="widen")
        after = [to_z]
        held.append(z_flip(to_z, step))
        places = places + [(len(held) - 1, (i,)) for i in range(len(places))]
        offsets = offsets + [z ^ step for z in offsets]
        step //= 2

    outs = [(one, [(whole, pair(0, 1, 0) + [(2 + y, whole) for y in others])])]
    outs += [(one, [(whole, pair(1, 0, y) + [(2, (y - 1,))])]) for y in others]
    last_x, *last_y = add_up(outs, [kept1, got1, diag_x, *diag_y], after, name="stage2")
    after = last_x
    last_x = x_flip(last_x)
    last_y = [y_flip(d, y) for y, d in zip(others, last_y)]

    sums = [
        pair(0, 0, 0) + [(2 + y, whole) for y in others],
        pair(1, 0, 0) + [(2, whole)],
    ]
    outs = [((2, *one), [((h,), sums[h]) for h in range(2)])]
    (base,) = add_up(outs, [kept1, got1, side_x, *side_y], [after], name="sides", kind=F32)

    outs = [(one, [((z,), [(a, i + (h,))]) for z, (a, i) in zip(offsets, places)]) for h in range(2)]
    own = list(add_up(outs, held, [base], name="own"))
    on_x = [x_flip(own[0])]
    on_y = [[None, y_flip(own[1], y)] for y in others]
    on_x.append(x_flip(own[1]))
    for y in others:
        on_y[y - 1][0] = y_flip(own[0], y)
    diag = [[y_flip(on_x[0], y), x_flip(on_y[y - 1][1])] for y in others]

    arrays = [base, last_x, *last_y]
    plane = [[(0, (0,)), (1, ())], [(0, (1,))] + [(1 + y, ()) for y in others]]
    left = list(range(zs))
    sums = {(z, h): [(a, i + (z,)) for a, i in plane[h]] for z in left for h in range(2)}
    after = [own[0]]
    step = 1
    while step < zs:
        going = [z for z in left if z & step]
        left = [z for z in left if not z & step]
        outs = [((len(going), 2, rows, half), [((i, h), sums[z, h]) for i, z in enumerate(going) for h in range(2)])]
        (to_z,) = add_up(outs, arrays, after, name="plane")
        arrays = [*arrays, z_flip(to_z, step)]
        after = [to_z]
        sums = {(z, h): sums[z, h] + [(len(arrays) - 1, (i, h))] for i, z in enumerate(left) for h in range(2)}
        step *= 2
    weight_grad = finish([sums[0, 0], sums[0, 1]], arrays, tokens)

    held = own + [e for es in on_y for e in es] + on_x
    groups = [range(2 * ys), range(2 * ys, 2 * ys + 2)]
    outs = [((len(g), *one), [((i - g[0],), [(i, whole)]) for i in g]) for g in groups]
    near, side = add_up(outs, held, name="most")
    ends = [d for ds in diag for d in ds]
    near = [near, core_flip(near)]
    far = [side, *ends, core_flip(side), *[core_flip(e) for e in ends]]
    projected = make_project(tokens, near, far, ys, zs)
    return projected, weight_grad.T


def solution(mesh):
    placed = (
        P(("wide", "node"), None),
        P("wide", "node"),
        P(None, "node"),
        P(("wide", "node"), None),
    )
    return jax.shard_map(
        functools.partial(on_device, mesh.shape["wide"], mesh.shape["node"]),
        mesh=mesh,
        in_specs=placed,
        out_specs=(P(("wide", "node"), None), P("wide", "node")),
        check_vma=False,
    )
```

```python
import functools

import jax
import jax.numpy as jnp
from jax import lax
from jax.experimental import pallas as pl
from jax.experimental.pallas import tpu as pltpu
from jax.sharding import PartitionSpec as P

BLOCK = 128
F32 = jnp.float32
BF16 = jnp.bfloat16
NT = (((1,), (1,)), ((), ()))
VMEM = pl.BlockSpec(memory_space=pltpu.VMEM)
ANY = pl.BlockSpec(memory_space=pl.ANY)
PARAMS = pltpu.CompilerParams(vmem_limit_bytes=10 << 20)


def place_of(h, x, y, ys):
    return 2 * (ys * x + y) + h


def turn_of(h, x, y, ys):
    if x and y:
        return 0, 2 * (y - 1) + h
    if (x and h) or (y and not h):
        return 0, 2 * (ys - 1) + y
    return 1, (2 + y if x or y else h)


def flip(entries, axis, offset, size):
    return lax.ppermute(entries, axis, [(i, i ^ offset) for i in range(size)])


def columns_of(x, z, cols):
    place = lax.bitwise_xor(lax.axis_index("wide"), 2 * z + x) * cols
    return pl.ds(pl.multiple_of(place, cols), cols)


def first_kernel(ys, zs, tokens, cot, codes, scales, *refs):
    (*made, weight, tokens_v, cot_v, codes_v, scales_v, cot_t, sems) = refs
    rows, cols = codes.shape
    half = cols // 2
    fetched = []

    def fetch(src, dst):
        fetched.append(pltpu.make_async_copy(src, dst, sems.at[len(fetched)]))
        fetched[-1].start()

    for src, dst in ((cot, cot_v), (codes, codes_v), (scales, scales_v)):
        fetch(src, dst)
    order = [(x, z) for x in (1, 0) for z in range(zs)]
    for x, z in order:
        place = columns_of(x, z, cols)
        fetch(tokens.at[:, place], tokens_v.at[:, place])
    for copy in fetched[:3]:
        copy.wait()

    blocks = cols // BLOCK
    first = lax.axis_index("wide") * blocks
    shape = (scales.shape[1], blocks)
    chosen = lax.broadcasted_iota(jnp.int32, shape, 0) == first + lax.broadcasted_iota(jnp.int32, shape, 1)
    factor = jnp.dot(scales_v[...], chosen.astype(F32).astype(BF16), preferred_element_type=F32)
    for b in range(blocks):
        at = b * BLOCK
        piece = (codes_v[:, at : at + BLOCK].astype(F32) * factor[:, b : b + 1]).astype(BF16)
        weight[at // half, :, at % half : at % half + BLOCK] = piece

    cot_t[...] = cot_v[...].astype(F32).T.astype(BF16)
    node = lax.axis_index("node")
    names = [(core, y) for core in (1, 0) for y in range(ys)]
    picked = []
    for core, y in names:
        place = lax.bitwise_xor(node, 2 * y + core) * rows
        picked.append(cot_t[pl.ds(pl.multiple_of(place, rows), rows), :])
    left = jnp.concatenate(picked, axis=0)
    for copy, (x, z) in zip(fetched[3:], order):
        copy.wait()
        right = tokens_v[:, columns_of(x, z, cols)]
        for h in range(2):
            part = jnp.dot(left, right[:, h * half : (h + 1) * half], preferred_element_type=F32).astype(BF16)
            for i, (core, y) in enumerate(names):
                turn, at = turn_of(h, x, y, ys)
                made[2 * (1 - core) + turn][at, z] = part[i * rows : (i + 1) * rows]


def local_products(tokens, cot, codes, scales, ys, zs):
    rows, cols = codes.shape
    half = cols // 2
    operands = (tokens, cot, codes, scales)
    blocks = [jax.ShapeDtypeStruct((n, zs, rows, half), BF16) for n in (3 * ys - 2, ys + 2)]
    return pl.pallas_call(
        functools.partial(first_kernel, ys, zs),
        out_shape=(*blocks, *blocks, jax.ShapeDtypeStruct((2, rows, half), BF16)),
        in_specs=[ANY] * 4,
        out_specs=(VMEM,) * 5,
        scratch_shapes=[pltpu.VMEM(a.shape, BF16) for a in operands]
        + [pltpu.VMEM(cot.shape[::-1], BF16), pltpu.SemaphoreType.DMA((3 + 2 * zs,))],
        compiler_params=PARAMS,
        cost_estimate=pl.CostEstimate(
            flops=2 * tokens.size * cot.shape[1], bytes_accessed=4 * tokens.size, transcendentals=0
        ),
        name="first",
    )(*[pltpu.with_memory_space_constraint(a, pltpu.HBM) for a in operands])


def plain_products(tokens, cot, codes, scales, ys, zs):
    rows, cols = codes.shape
    half = cols // 2
    node, wide = lax.axis_index("node"), lax.axis_index("wide")
    part = jnp.dot(cot.T, tokens, preferred_element_type=F32).astype(BF16)
    part = part.reshape(2 * ys, rows, 2 * zs, 2, half).transpose(3, 0, 2, 1, 4)
    part = jnp.take(part, jnp.arange(2 * ys) ^ node, axis=1)
    part = jnp.take(part, jnp.arange(2 * zs) ^ wide, axis=2)
    part = part.reshape(2, ys, 2, zs, 2, rows, half).transpose(2, 4, 1, 0, 3, 5, 6)
    part = part.reshape(2, 4 * ys, zs, rows, half)
    split = []
    for core in (1, 0):
        named = {turn_of(h, x, y, ys): part[core, place_of(h, x, y, ys)] for h in range(2) for x in range(2) for y in range(ys)}
        for turn, count in enumerate((3 * ys - 2, ys + 2)):
            split.append(jnp.stack([named[turn, i] for i in range(count)]))
    index = (wide * cols + jnp.arange(cols)) // BLOCK
    factor = jnp.take(scales, index, axis=1).astype(F32)
    weight = (codes.astype(F32) * factor).astype(BF16)
    weight = weight.reshape(rows, 2, half).transpose(1, 0, 2)
    return *split, weight


def add_up(outs, arrays, after=(), name="add_up", kind=BF16):
    shapes = [jax.ShapeDtypeStruct(shape, kind) for shape, _ in outs]
    rows, half = arrays[0].shape[-2:]
    if half % BLOCK or rows % 16:
        results = []
        for shape, places in outs:
            result = jnp.zeros(shape, kind)
            for at, terms in places:
                total = sum(arrays[a][i].astype(F32) for a, i in terms)
                result = result.at[at].set(total.astype(kind))
            results.append(result)
        return results

    def kernel(*refs):
        given, made = refs[: len(arrays)], refs[len(arrays) + len(after) :]
        for out, (_, places) in zip(made, outs):
            for at, terms in places:
                terms = [given[a][i] for a, i in terms]
                if len(terms) > 1:
                    terms = [sum(t.astype(F32) for t in terms).astype(kind)]
                out[at] = terms[0]

    return pl.pallas_call(
        kernel,
        out_shape=shapes,
        in_specs=[VMEM] * len(arrays) + [ANY] * len(after),
        out_specs=[VMEM] * len(outs),
        compiler_params=PARAMS,
        name=name,
    )(*arrays, *after)


def finish(sums, arrays, after):
    rows, half = arrays[0].shape[-2:]

    def total(given, h):
        return sum(given[a][i].astype(F32) for a, i in sums[h])

    if half % BLOCK or rows % 16:
        return jnp.concatenate([total(arrays, h) for h in range(2)], axis=1)

    def kernel(*refs):
        for h in range(2):
            refs[-1][:, h * half : (h + 1) * half] = total(refs[:-2], h)

    return pl.pallas_call(
        kernel,
        out_shape=jax.ShapeDtypeStruct((rows, 2 * half), F32),
        in_specs=[VMEM] * len(arrays) + [ANY],
        out_specs=VMEM,
        compiler_params=PARAMS,
        cost_estimate=pl.CostEstimate(flops=4 * 10**10, bytes_accessed=1, transcendentals=0),
        name="finish",
    )(*arrays, after)


def project_kernel(ys, zs, x, tokens, *refs):
    if x == 0:
        (*weights, out) = refs
        total = 0.0
    else:
        (*weights, earlier, grad, out, grad_out, total_t, sem) = refs
        total = earlier[...]
        copy = pltpu.make_async_copy(grad, grad_out, sem)
        copy.start()
    count = len(weights) // 2
    rows, half = weights[0].shape[2:]
    cols = 2 * half
    for z in range(zs):
        pieces = tokens[:, columns_of(x, z, cols)]
        for h in range(2):
            picked = []
            for n in range(2 * ys):
                held = weights[count * (n % 2) : count * (n % 2 + 1)]
                y = n // 2
                if x and y:
                    picked.append(held[1 + 2 * (y - 1) + 1 - h][z])
                else:
                    picked.append(held[0][2 * y + h, z])
            left = jnp.concatenate(picked, axis=0)
            right = pieces[:, h * half : (h + 1) * half]
            total = total + lax.dot_general(left, right, NT, preferred_element_type=F32)
    if x == 0:
        out[...] = total
        return
    node = lax.axis_index("node")
    total_t[...] = total.reshape(total_t.shape)
    ordered = [total_t[lax.bitwise_xor(node, n)] for n in range(2 * ys)]
    out[...] = jnp.concatenate(ordered, axis=0).T.astype(BF16)
    copy.wait()


def project(tokens, near, far, grad, ys, zs):
    rows = near[0].shape[2]
    count, width = tokens.shape[0], 2 * ys * rows
    cost = pl.CostEstimate(flops=tokens.size * width, bytes_accessed=2 * tokens.size, transcendentals=0)
    earlier = pl.pallas_call(
        functools.partial(project_kernel, ys, zs, 0),
        out_shape=jax.ShapeDtypeStruct((width, count), F32),
        in_specs=[VMEM] * (1 + len(near)),
        out_specs=VMEM,
        compiler_params=PARAMS,
        cost_estimate=cost,
        name="project_near",
    )(tokens, *near)
    return pl.pallas_call(
        functools.partial(project_kernel, ys, zs, 1),
        out_shape=(jax.ShapeDtypeStruct((count, width), BF16), jax.ShapeDtypeStruct(grad.shape, F32)),
        in_specs=[VMEM] * (3 + len(far)),
        out_specs=(VMEM, ANY),
        scratch_shapes=[pltpu.VMEM((2 * ys, rows, count), F32), pltpu.SemaphoreType.DMA],
        compiler_params=PARAMS,
        cost_estimate=cost,
        name="project_far",
    )(tokens, *far, earlier, grad)


def plain_project(tokens, near, far, grad, ys, zs):
    rows, half = near[0].shape[2:]
    node, wide = lax.axis_index("node"), lax.axis_index("wide")
    pieces = tokens.reshape(tokens.shape[0], 2 * zs, 2, half)
    pieces = jnp.take(pieces, jnp.arange(2 * zs) ^ wide, axis=1)
    pieces = pieces.reshape(tokens.shape[0], zs, 2, 2, half)
    count = len(far) // 2
    weights = [
        jnp.concatenate(
            [near[c], far[count * c]]
            + [far[count * c + 1 + 2 * y + 1 - h][None] for y in range(ys - 1) for h in range(2)]
        )
        for c in range(2)
    ]
    total = []
    for n in range(2 * ys):
        part = 0.0
        for h in range(2):
            for x in range(2):
                held = weights[n % 2][place_of(h, x, n // 2, ys)]
                part = part + jnp.einsum("tzl,zrl->tr", pieces[:, :, x, h], held, preferred_element_type=F32)
        total.append(part)
    total = jnp.take(jnp.stack(total, axis=1), jnp.arange(2 * ys) ^ node, axis=1)
    return total.reshape(tokens.shape[0], -1).astype(BF16), grad


def on_device(wides, nodes, tokens, codes, scales, cotangent):
    ys, zs = nodes // 2, wides // 2
    cols, rows = codes.shape
    half = cols // 2
    aligned = half % BLOCK == 0 and rows % 16 == 0
    products, make_project = (local_products, project) if aligned else (plain_products, plain_project)
    others = range(1, ys)
    one = (zs, rows, half)
    whole = (...,)

    def core_flip(entries):
        return flip(entries, "node", 1, nodes)

    def y_flip(entries, y):
        return flip(entries, "node", 2 * y, nodes)

    def x_flip(entries):
        return flip(entries, "wide", 1, wides)

    def z_flip(entries, z):
        return flip(entries, "wide", 2 * z, wides)

    sent0, sent1, kept0, kept1, weight = products(tokens, cotangent, codes.T, scales.T, ys, zs)

    got0, got1 = core_flip(sent0), core_flip(sent1)
    held = [weight, z_flip(weight, zs // 2)]
    offsets = [0, zs // 2]
    places = [(0, ()), (1, ())]

    def pair(h, x, y):
        _, at = turn_of(h, x, y, ys)
        return [(0, (at,)), (1, (at,))]

    outs = [((ys - 1, *one), [((y - 1,), pair(1, 1, y)) for y in others])]
    outs += [(one, [(whole, pair(0, 1, y))]) for y in others]
    outs += [(one, [(whole, pair(1, 1, 0))])]
    outs += [(one, [(whole, pair(0, 0, y))]) for y in others]
    diag_x, *rest = add_up(outs, [kept0, got0], name="stage1")
    after = [diag_x]
    diag_y, side_x, side_y = rest[: ys - 1], rest[ys - 1], rest[ys:]
    diag_x = x_flip(diag_x)
    diag_y = [y_flip(d, y) for y, d in zip(others, diag_y)]
    side_x = x_flip(side_x)
    side_y = [y_flip(d, y) for y, d in zip(others, side_y)]

    step = zs // 4
    while step:
        outs = [((len(places), 2, rows, half), [((i,), [place]) for i, place in enumerate(places)])]
        (to_z,) = add_up(outs, held, after, name="widen")
        after = [to_z]
        held.append(z_flip(to_z, step))
        places = places + [(len(held) - 1, (i,)) for i in range(len(places))]
        offsets = offsets + [z ^ step for z in offsets]
        step //= 2

    outs = [(one, [(whole, pair(0, 1, 0) + [(2 + y, whole) for y in others])])]
    outs += [(one, [(whole, pair(1, 0, y) + [(2, (y - 1,))])]) for y in others]
    last_x, *last_y = add_up(outs, [kept1, got1, diag_x, *diag_y], after, name="stage2")
    after = last_x
    last_x = x_flip(last_x)
    last_y = [y_flip(d, y) for y, d in zip(others, last_y)]

    sums = [
        pair(0, 0, 0) + [(2 + y, whole) for y in others],
        pair(1, 0, 0) + [(2, whole)],
    ]
    outs = [((2, *one), [((h,), sums[h]) for h in range(2)])]
    (base,) = add_up(outs, [kept1, got1, side_x, *side_y], [after], name="sides", kind=F32)

    outs = [(one, [((z,), [(a, i + (h,))]) for z, (a, i) in zip(offsets, places)]) for h in range(2)]
    own = list(add_up(outs, held, [base], name="own"))
    on_x = [x_flip(own[0])]
    on_y = [[None, y_flip(own[1], y)] for y in others]
    on_x.append(x_flip(own[1]))
    for y in others:
        on_y[y - 1][0] = y_flip(own[0], y)
    diag = [[y_flip(on_x[0], y), x_flip(on_y[y - 1][1])] for y in others]

    arrays = [base, last_x, *last_y]
    plane = [[(0, (0,)), (1, ())], [(0, (1,))] + [(1 + y, ()) for y in others]]
    left = list(range(zs))
    sums = {(z, h): [(a, i + (z,)) for a, i in plane[h]] for z in left for h in range(2)}
    after = [own[0]]
    step = 1
    while step < zs:
        going = [z for z in left if z & step]
        left = [z for z in left if not z & step]
        outs = [((len(going), 2, rows, half), [((i, h), sums[z, h]) for i, z in enumerate(going) for h in range(2)])]
        (to_z,) = add_up(outs, arrays, after, name="plane")
        arrays = [*arrays, z_flip(to_z, step)]
        after = [to_z]
        sums = {(z, h): sums[z, h] + [(len(arrays) - 1, (i, h))] for i, z in enumerate(left) for h in range(2)}
        step *= 2
    weight_grad = finish([sums[0, 0], sums[0, 1]], arrays, tokens)

    held = own + [e for es in on_y for e in es] + on_x
    groups = [range(2 * ys), range(2 * ys, 2 * ys + 2)]
    outs = [((len(g), *one), [((i - g[0],), [(i, whole)]) for i in g]) for g in groups]
    near, side = add_up(outs, held, name="most")
    ends = [d for ds in diag for d in ds[::-1]]
    near = [near, core_flip(near)]
    far = [side, *ends, core_flip(side), *[core_flip(e) for e in ends]]
    projected, weight_grad = make_project(tokens, near, far, weight_grad, ys, zs)
    return projected, weight_grad.T


def solution(mesh):
    placed = (
        P(("wide", "node"), None),
        P("wide", "node"),
        P(None, "node"),
        P(("wide", "node"), None),
    )
    return jax.shard_map(
        functools.partial(on_device, mesh.shape["wide"], mesh.shape["node"]),
        mesh=mesh,
        in_specs=placed,
        out_specs=(P(("wide", "node"), None), P("wide", "node")),
        check_vma=False,
    )
```

```python
import functools

import jax
import jax.numpy as jnp
from jax import lax
from jax.experimental import pallas as pl
from jax.experimental.pallas import tpu as pltpu
from jax.sharding import PartitionSpec as P

BLOCK = 128
F32 = jnp.float32
BF16 = jnp.bfloat16
NT = (((1,), (1,)), ((), ()))
VMEM = pl.BlockSpec(memory_space=pltpu.VMEM)
ANY = pl.BlockSpec(memory_space=pl.ANY)
PARAMS = pltpu.CompilerParams(vmem_limit_bytes=10 << 20)


def place_of(h, x, y, ys):
    return 2 * (ys * x + y) + h


def turn_of(h, x, y, ys):
    if x and y:
        return 0, 2 * (y - 1) + h
    if (x and h) or (y and not h):
        return 0, 2 * (ys - 1) + y
    return 1, (2 + y if x or y else h)


def flip(entries, axis, offset, size):
    return lax.ppermute(entries, axis, [(i, i ^ offset) for i in range(size)])


def columns_of(x, z, cols):
    place = lax.bitwise_xor(lax.axis_index("wide"), 2 * z + x) * cols
    return pl.ds(pl.multiple_of(place, cols), cols)


def first_kernel(ys, zs, tokens, cot, codes, scales, *refs):
    (*made, weight, tokens_v, cot_v, codes_v, scales_v, cot_t, sems) = refs
    rows, cols = codes.shape
    half = cols // 2
    fetched = []

    def fetch(src, dst):
        fetched.append(pltpu.make_async_copy(src, dst, sems.at[len(fetched)]))
        fetched[-1].start()

    for src, dst in ((cot, cot_v), (codes, codes_v), (scales, scales_v)):
        fetch(src, dst)
    order = [(x, z) for x in (1, 0) for z in range(zs)]
    for x, z in order:
        place = columns_of(x, z, cols)
        fetch(tokens.at[:, place], tokens_v.at[:, place])
    for copy in fetched[:3]:
        copy.wait()

    blocks = cols // BLOCK
    first = lax.axis_index("wide") * blocks
    shape = (scales.shape[1], blocks)
    chosen = lax.broadcasted_iota(jnp.int32, shape, 0) == first + lax.broadcasted_iota(jnp.int32, shape, 1)
    factor = jnp.dot(scales_v[...], chosen.astype(F32).astype(BF16), preferred_element_type=F32)
    for b in range(blocks):
        at = b * BLOCK
        piece = (codes_v[:, at : at + BLOCK].astype(F32) * factor[:, b : b + 1]).astype(BF16)
        weight[at // half, :, at % half : at % half + BLOCK] = piece

    cot_t[...] = cot_v[...].astype(F32).T.astype(BF16)
    node = lax.axis_index("node")
    names = [(core, y) for core in (1, 0) for y in range(ys)]
    picked = []
    for core, y in names:
        place = lax.bitwise_xor(node, 2 * y + core) * rows
        picked.append(cot_t[pl.ds(pl.multiple_of(place, rows), rows), :])
    left = jnp.concatenate(picked, axis=0)
    for copy, (x, z) in zip(fetched[3:], order):
        copy.wait()
        right = tokens_v[:, columns_of(x, z, cols)]
        for h in range(2):
            part = jnp.dot(left, right[:, h * half : (h + 1) * half], preferred_element_type=F32).astype(BF16)
            for i, (core, y) in enumerate(names):
                turn, at = turn_of(h, x, y, ys)
                made[2 * (1 - core) + turn][at, z] = part[i * rows : (i + 1) * rows]


def local_products(tokens, cot, codes, scales, ys, zs):
    rows, cols = codes.shape
    half = cols // 2
    operands = (tokens, cot, codes, scales)
    blocks = [jax.ShapeDtypeStruct((n, zs, rows, half), BF16) for n in (3 * ys - 2, ys + 2)]
    return pl.pallas_call(
        functools.partial(first_kernel, ys, zs),
        out_shape=(*blocks, *blocks, jax.ShapeDtypeStruct((2, rows, half), BF16)),
        in_specs=[ANY] * 4,
        out_specs=(VMEM,) * 5,
        scratch_shapes=[pltpu.VMEM(a.shape, BF16) for a in operands]
        + [pltpu.VMEM(cot.shape[::-1], BF16), pltpu.SemaphoreType.DMA((3 + 2 * zs,))],
        compiler_params=PARAMS,
        cost_estimate=pl.CostEstimate(
            flops=2 * tokens.size * cot.shape[1], bytes_accessed=4 * tokens.size, transcendentals=0
        ),
        name="first",
    )(*[pltpu.with_memory_space_constraint(a, pltpu.HBM) for a in operands])


def plain_products(tokens, cot, codes, scales, ys, zs):
    rows, cols = codes.shape
    half = cols // 2
    node, wide = lax.axis_index("node"), lax.axis_index("wide")
    part = jnp.dot(cot.T, tokens, preferred_element_type=F32).astype(BF16)
    part = part.reshape(2 * ys, rows, 2 * zs, 2, half).transpose(3, 0, 2, 1, 4)
    part = jnp.take(part, jnp.arange(2 * ys) ^ node, axis=1)
    part = jnp.take(part, jnp.arange(2 * zs) ^ wide, axis=2)
    part = part.reshape(2, ys, 2, zs, 2, rows, half).transpose(2, 4, 1, 0, 3, 5, 6)
    part = part.reshape(2, 4 * ys, zs, rows, half)
    split = []
    for core in (1, 0):
        named = {turn_of(h, x, y, ys): part[core, place_of(h, x, y, ys)] for h in range(2) for x in range(2) for y in range(ys)}
        for turn, count in enumerate((3 * ys - 2, ys + 2)):
            split.append(jnp.stack([named[turn, i] for i in range(count)]))
    index = (wide * cols + jnp.arange(cols)) // BLOCK
    factor = jnp.take(scales, index, axis=1).astype(F32)
    weight = (codes.astype(F32) * factor).astype(BF16)
    weight = weight.reshape(rows, 2, half).transpose(1, 0, 2)
    return *split, weight


def add_up(outs, arrays, after=(), name="add_up", kind=BF16):
    shapes = [jax.ShapeDtypeStruct(shape, kind) for shape, _ in outs]
    rows, half = arrays[0].shape[-2:]
    if half % BLOCK or rows % 16:
        results = []
        for shape, places in outs:
            result = jnp.zeros(shape, kind)
            for at, terms in places:
                total = sum(arrays[a][i].astype(F32) for a, i in terms)
                result = result.at[at].set(total.astype(kind))
            results.append(result)
        return results

    def kernel(*refs):
        given, made = refs[: len(arrays)], refs[len(arrays) + len(after) :]
        for out, (_, places) in zip(made, outs):
            for at, terms in places:
                terms = [given[a][i] for a, i in terms]
                if len(terms) > 1:
                    terms = [sum(t.astype(F32) for t in terms).astype(kind)]
                out[at] = terms[0]

    return pl.pallas_call(
        kernel,
        out_shape=shapes,
        in_specs=[VMEM] * len(arrays) + [ANY] * len(after),
        out_specs=[VMEM] * len(outs),
        compiler_params=PARAMS,
        name=name,
    )(*arrays, *after)


def finish(sums, arrays, after):
    rows, half = arrays[0].shape[-2:]

    def total(given, h):
        return sum(given[a][i].astype(F32) for a, i in sums[h])

    if half % BLOCK or rows % 16:
        return jnp.concatenate([total(arrays, h) for h in range(2)], axis=1)

    def kernel(*refs):
        for h in range(2):
            refs[-1][:, h * half : (h + 1) * half] = total(refs[:-2], h)

    return pl.pallas_call(
        kernel,
        out_shape=jax.ShapeDtypeStruct((rows, 2 * half), F32),
        in_specs=[VMEM] * len(arrays) + [ANY],
        out_specs=VMEM,
        compiler_params=PARAMS,
        cost_estimate=pl.CostEstimate(flops=4 * 10**10, bytes_accessed=1, transcendentals=0),
        name="finish",
    )(*arrays, after)


def project_kernel(ys, zs, x, tokens, *refs):
    if x == 0:
        (*weights, out) = refs
        total = 0.0
    else:
        (*weights, earlier, grad, out, grad_out, total_t, sem) = refs
        total = earlier[...]
        copy = pltpu.make_async_copy(grad, grad_out, sem)
        copy.start()
    count = len(weights) // 2
    rows, half = weights[0].shape[2:]
    cols = 2 * half
    for z in range(zs):
        pieces = tokens[:, columns_of(x, z, cols)]
        for h in range(2):
            picked = []
            for n in range(2 * ys):
                held = weights[count * (n % 2) : count * (n % 2 + 1)]
                y = n // 2
                if x and y:
                    picked.append(held[1 + 2 * (y - 1) + h][z])
                else:
                    picked.append(held[0][2 * y + h, z])
            left = jnp.concatenate(picked, axis=0)
            right = pieces[:, h * half : (h + 1) * half]
            total = total + lax.dot_general(left, right, NT, preferred_element_type=F32)
    if x == 0:
        out[...] = total
        return
    node = lax.axis_index("node")
    total_t[...] = total.reshape(total_t.shape)
    ordered = [total_t[lax.bitwise_xor(node, n)] for n in range(2 * ys)]
    out[...] = jnp.concatenate(ordered, axis=0).T.astype(BF16)
    copy.wait()


def project(tokens, near, far, grad, ys, zs):
    rows = near[0].shape[2]
    count, width = tokens.shape[0], 2 * ys * rows
    cost = pl.CostEstimate(flops=tokens.size * width, bytes_accessed=2 * tokens.size, transcendentals=0)
    earlier = pl.pallas_call(
        functools.partial(project_kernel, ys, zs, 0),
        out_shape=jax.ShapeDtypeStruct((width, count), F32),
        in_specs=[VMEM] * (1 + len(near)),
        out_specs=VMEM,
        compiler_params=PARAMS,
        cost_estimate=cost,
        name="project_near",
    )(tokens, *near)
    return pl.pallas_call(
        functools.partial(project_kernel, ys, zs, 1),
        out_shape=(jax.ShapeDtypeStruct((count, width), BF16), jax.ShapeDtypeStruct(grad.shape, F32)),
        in_specs=[VMEM] * (3 + len(far)),
        out_specs=(VMEM, ANY),
        scratch_shapes=[pltpu.VMEM((2 * ys, rows, count), F32), pltpu.SemaphoreType.DMA],
        compiler_params=PARAMS,
        cost_estimate=cost,
        name="project_far",
    )(tokens, *far, earlier, grad)


def plain_project(tokens, near, far, grad, ys, zs):
    rows, half = near[0].shape[2:]
    node, wide = lax.axis_index("node"), lax.axis_index("wide")
    pieces = tokens.reshape(tokens.shape[0], 2 * zs, 2, half)
    pieces = jnp.take(pieces, jnp.arange(2 * zs) ^ wide, axis=1)
    pieces = pieces.reshape(tokens.shape[0], zs, 2, 2, half)
    count = len(far) // 2
    weights = [
        jnp.concatenate([near[c], far[count * c], jnp.stack(far[count * c + 1 : count * (c + 1)])]) for c in range(2)
    ]
    total = []
    for n in range(2 * ys):
        part = 0.0
        for h in range(2):
            for x in range(2):
                held = weights[n % 2][place_of(h, x, n // 2, ys)]
                part = part + jnp.einsum("tzl,zrl->tr", pieces[:, :, x, h], held, preferred_element_type=F32)
        total.append(part)
    total = jnp.take(jnp.stack(total, axis=1), jnp.arange(2 * ys) ^ node, axis=1)
    return total.reshape(tokens.shape[0], -1).astype(BF16), grad


def on_device(wides, nodes, tokens, codes, scales, cotangent):
    ys, zs = nodes // 2, wides // 2
    cols, rows = codes.shape
    half = cols // 2
    aligned = half % BLOCK == 0 and rows % 16 == 0
    products, make_project = (local_products, project) if aligned else (plain_products, plain_project)
    others = range(1, ys)
    one = (zs, rows, half)
    whole = (...,)

    def core_flip(entries):
        return flip(entries, "node", 1, nodes)

    def y_flip(entries, y):
        return flip(entries, "node", 2 * y, nodes)

    def x_flip(entries):
        return flip(entries, "wide", 1, wides)

    def z_flip(entries, z):
        return flip(entries, "wide", 2 * z, wides)

    sent0, sent1, kept0, kept1, weight = products(tokens, cotangent, codes.T, scales.T, ys, zs)

    got0, got1 = core_flip(sent0), core_flip(sent1)
    held = [weight, z_flip(weight, zs // 2)]
    offsets = [0, zs // 2]
    places = [(0, ()), (1, ())]

    def pair(h, x, y):
        _, at = turn_of(h, x, y, ys)
        return [(0, (at,)), (1, (at,))]

    outs = [((ys - 1, *one), [((y - 1,), pair(1, 1, y)) for y in others])]
    outs += [(one, [(whole, pair(0, 1, y))]) for y in others]
    outs += [(one, [(whole, pair(1, 1, 0))])]
    outs += [(one, [(whole, pair(0, 0, y))]) for y in others]
    diag_x, *rest = add_up(outs, [kept0, got0], name="stage1")
    after = [diag_x]
    diag_y, side_x, side_y = rest[: ys - 1], rest[ys - 1], rest[ys:]
    diag_x = x_flip(diag_x)
    diag_y = [y_flip(d, y) for y, d in zip(others, diag_y)]
    side_x = x_flip(side_x)
    side_y = [y_flip(d, y) for y, d in zip(others, side_y)]

    step = zs // 4
    while step:
        outs = [((len(places), 2, rows, half), [((i,), [place]) for i, place in enumerate(places)])]
        (to_z,) = add_up(outs, held, after, name="widen")
        after = [to_z]
        held.append(z_flip(to_z, step))
        places = places + [(len(held) - 1, (i,)) for i in range(len(places))]
        offsets = offsets + [z ^ step for z in offsets]
        step //= 2

    outs = [(one, [(whole, pair(0, 1, 0) + [(2 + y, whole) for y in others])])]
    outs += [(one, [(whole, pair(1, 0, y) + [(2, (y - 1,))])]) for y in others]
    last_x, *last_y = add_up(outs, [kept1, got1, diag_x, *diag_y], after, name="stage2")
    after = last_x
    last_x = x_flip(last_x)
    last_y = [y_flip(d, y) for y, d in zip(others, last_y)]

    sums = [
        pair(0, 0, 0) + [(2 + y, whole) for y in others],
        pair(1, 0, 0) + [(2, whole)],
    ]
    outs = [((2, *one), [((h,), sums[h]) for h in range(2)])]
    (base,) = add_up(outs, [kept1, got1, side_x, *side_y], [after], name="sides", kind=F32)

    outs = [(one, [((z,), [(a, i + (h,))]) for z, (a, i) in zip(offsets, places)]) for h in range(2)]
    own = list(add_up(outs, held, [base], name="own"))
    on_x = [x_flip(own[0])]
    on_y = [[None, y_flip(own[1], y)] for y in others]
    on_x.append(x_flip(own[1]))
    for y in others:
        on_y[y - 1][0] = y_flip(own[0], y)
    diag = [[y_flip(on_x[0], y), x_flip(on_y[y - 1][1])] for y in others]

    arrays = [base, last_x, *last_y]
    plane = [[(0, (0,)), (1, ())], [(0, (1,))] + [(1 + y, ()) for y in others]]
    left = list(range(zs))
    sums = {(z, h): [(a, i + (z,)) for a, i in plane[h]] for z in left for h in range(2)}
    after = [own[0]]
    step = 1
    while step < zs:
        going = [z for z in left if z & step]
        left = [z for z in left if not z & step]
        outs = [((len(going), 2, rows, half), [((i, h), sums[z, h]) for i, z in enumerate(going) for h in range(2)])]
        (to_z,) = add_up(outs, arrays, after, name="plane")
        arrays = [*arrays, z_flip(to_z, step)]
        after = [to_z]
        sums = {(z, h): sums[z, h] + [(len(arrays) - 1, (i, h))] for i, z in enumerate(left) for h in range(2)}
        step *= 2
    weight_grad = finish([sums[0, 0], sums[0, 1]], arrays, tokens)

    held = own + [e for es in on_y for e in es] + on_x
    groups = [range(2 * ys), range(2 * ys, 2 * ys + 2)]
    outs = [((len(g), *one), [((i - g[0],), [(i, whole)]) for i in g]) for g in groups]
    near, side = add_up(outs, held, name="most")
    ends = [d for ds in diag for d in ds]
    near = [near, core_flip(near)]
    far = [side, *ends, core_flip(side), *[core_flip(e) for e in ends]]
    projected, weight_grad = make_project(tokens, near, far, weight_grad, ys, zs)
    return projected, weight_grad.T


def solution(mesh):
    placed = (
        P(("wide", "node"), None),
        P("wide", "node"),
        P(None, "node"),
        P(("wide", "node"), None),
    )
    return jax.shard_map(
        functools.partial(on_device, mesh.shape["wide"], mesh.shape["node"]),
        mesh=mesh,
        in_specs=placed,
        out_specs=(P(("wide", "node"), None), P("wide", "node")),
        check_vma=False,
    )
```

```python
import functools

import jax
import jax.numpy as jnp
from jax import lax
from jax.experimental import pallas as pl
from jax.experimental.pallas import tpu as pltpu
from jax.sharding import PartitionSpec as P

BLOCK = 128
F32 = jnp.float32
BF16 = jnp.bfloat16
NT = (((1,), (1,)), ((), ()))
VMEM = pl.BlockSpec(memory_space=pltpu.VMEM)
ANY = pl.BlockSpec(memory_space=pl.ANY)
PARAMS = pltpu.CompilerParams(vmem_limit_bytes=10 << 20)


def place_of(h, x, y, ys):
    return 2 * (ys * x + y) + h


def turn_of(h, x, y, ys):
    if x and y:
        return 0, 2 * (y - 1) + h
    if (x and h) or (y and not h):
        return 0, 2 * (ys - 1) + y
    return 1, (2 + y if x or y else h)


def flip(entries, axis, offset, size):
    return lax.ppermute(entries, axis, [(i, i ^ offset) for i in range(size)])


def columns_of(x, z, cols):
    place = lax.bitwise_xor(lax.axis_index("wide"), 2 * z + x) * cols
    return pl.ds(pl.multiple_of(place, cols), cols)


def first_kernel(ys, zs, tokens, cot, codes, scales, *refs):
    (*made, weight, tokens_v, cot_v, codes_v, scales_v, cot_t, sems) = refs
    rows, cols = codes.shape
    half = cols // 2
    fetched = []

    def fetch(src, dst):
        fetched.append(pltpu.make_async_copy(src, dst, sems.at[len(fetched)]))
        fetched[-1].start()

    for src, dst in ((cot, cot_v), (codes, codes_v), (scales, scales_v)):
        fetch(src, dst)
    order = [(x, z) for x in (1, 0) for z in range(zs)]
    for x, z in order:
        place = columns_of(x, z, cols)
        fetch(tokens.at[:, place], tokens_v.at[:, place])
    for copy in fetched[:3]:
        copy.wait()

    blocks = cols // BLOCK
    first = lax.axis_index("wide") * blocks
    shape = (scales.shape[1], blocks)
    chosen = lax.broadcasted_iota(jnp.int32, shape, 0) == first + lax.broadcasted_iota(jnp.int32, shape, 1)
    factor = jnp.dot(scales_v[...], chosen.astype(F32).astype(BF16), preferred_element_type=F32)
    for b in range(blocks):
        at = b * BLOCK
        piece = (codes_v[:, at : at + BLOCK].astype(F32) * factor[:, b : b + 1]).astype(BF16)
        weight[at // half, :, at % half : at % half + BLOCK] = piece

    cot_t[...] = cot_v[...].astype(F32).T.astype(BF16)
    node = lax.axis_index("node")
    names = [(core, y) for core in (1, 0) for y in range(ys)]
    picked = []
    for core, y in names:
        place = lax.bitwise_xor(node, 2 * y + core) * rows
        picked.append(cot_t[pl.ds(pl.multiple_of(place, rows), rows), :])
    left = jnp.concatenate(picked, axis=0)
    for copy, (x, z) in zip(fetched[3:], order):
        copy.wait()
        right = tokens_v[:, columns_of(x, z, cols)]
        for h in range(2):
            part = jnp.dot(left, right[:, h * half : (h + 1) * half], preferred_element_type=F32).astype(BF16)
            for i, (core, y) in enumerate(names):
                turn, at = turn_of(h, x, y, ys)
                made[2 * (1 - core) + turn][at, z] = part[i * rows : (i + 1) * rows]


def local_products(tokens, cot, codes, scales, ys, zs):
    rows, cols = codes.shape
    half = cols // 2
    operands = (tokens, cot, codes, scales)
    blocks = [jax.ShapeDtypeStruct((n, zs, rows, half), BF16) for n in (3 * ys - 2, ys + 2)]
    return pl.pallas_call(
        functools.partial(first_kernel, ys, zs),
        out_shape=(*blocks, *blocks, jax.ShapeDtypeStruct((2, rows, half), BF16)),
        in_specs=[ANY] * 4,
        out_specs=(VMEM,) * 5,
        scratch_shapes=[pltpu.VMEM(a.shape, BF16) for a in operands]
        + [pltpu.VMEM(cot.shape[::-1], BF16), pltpu.SemaphoreType.DMA((3 + 2 * zs,))],
        compiler_params=PARAMS,
        cost_estimate=pl.CostEstimate(
            flops=2 * tokens.size * cot.shape[1], bytes_accessed=4 * tokens.size, transcendentals=0
        ),
        name="first",
    )(*[pltpu.with_memory_space_constraint(a, pltpu.HBM) for a in operands])


def plain_products(tokens, cot, codes, scales, ys, zs):
    rows, cols = codes.shape
    half = cols // 2
    node, wide = lax.axis_index("node"), lax.axis_index("wide")
    part = jnp.dot(cot.T, tokens, preferred_element_type=F32).astype(BF16)
    part = part.reshape(2 * ys, rows, 2 * zs, 2, half).transpose(3, 0, 2, 1, 4)
    part = jnp.take(part, jnp.arange(2 * ys) ^ node, axis=1)
    part = jnp.take(part, jnp.arange(2 * zs) ^ wide, axis=2)
    part = part.reshape(2, ys, 2, zs, 2, rows, half).transpose(2, 4, 1, 0, 3, 5, 6)
    part = part.reshape(2, 4 * ys, zs, rows, half)
    split = []
    for core in (1, 0):
        named = {turn_of(h, x, y, ys): part[core, place_of(h, x, y, ys)] for h in range(2) for x in range(2) for y in range(ys)}
        for turn, count in enumerate((3 * ys - 2, ys + 2)):
            split.append(jnp.stack([named[turn, i] for i in range(count)]))
    index = (wide * cols + jnp.arange(cols)) // BLOCK
    factor = jnp.take(scales, index, axis=1).astype(F32)
    weight = (codes.astype(F32) * factor).astype(BF16)
    weight = weight.reshape(rows, 2, half).transpose(1, 0, 2)
    return *split, weight


def add_up(outs, arrays, after=(), name="add_up", kind=BF16):
    shapes = [jax.ShapeDtypeStruct(shape, kind) for shape, _ in outs]
    rows, half = arrays[0].shape[-2:]
    if half % BLOCK or rows % 16:
        results = []
        for shape, places in outs:
            result = jnp.zeros(shape, kind)
            for at, terms in places:
                total = sum(arrays[a][i].astype(F32) for a, i in terms)
                result = result.at[at].set(total.astype(kind))
            results.append(result)
        return results

    def kernel(*refs):
        given, made = refs[: len(arrays)], refs[len(arrays) + len(after) :]
        for out, (_, places) in zip(made, outs):
            for at, terms in places:
                terms = [given[a][i] for a, i in terms]
                if len(terms) > 1:
                    terms = [sum(t.astype(F32) for t in terms).astype(kind)]
                out[at] = terms[0]

    return pl.pallas_call(
        kernel,
        out_shape=shapes,
        in_specs=[VMEM] * len(arrays) + [ANY] * len(after),
        out_specs=[VMEM] * len(outs),
        compiler_params=PARAMS,
        name=name,
    )(*arrays, *after)


def finish(sums, arrays, after):
    rows, half = arrays[0].shape[-2:]

    def total(given, h):
        return sum(given[a][i].astype(F32) for a, i in sums[h])

    if half % BLOCK or rows % 16:
        return jnp.concatenate([total(arrays, h) for h in range(2)], axis=1)

    def kernel(*refs):
        for h in range(2):
            refs[-1][:, h * half : (h + 1) * half] = total(refs[:-2], h)

    return pl.pallas_call(
        kernel,
        out_shape=jax.ShapeDtypeStruct((rows, 2 * half), F32),
        in_specs=[VMEM] * len(arrays) + [ANY],
        out_specs=VMEM,
        compiler_params=PARAMS,
        cost_estimate=pl.CostEstimate(flops=4 * 10**10, bytes_accessed=1, transcendentals=0),
        name="finish",
    )(*arrays, after)


def project_kernel(ys, zs, x, tokens, *refs):
    if x == 0:
        (*weights, out) = refs
        total = 0.0
    else:
        (*weights, earlier, grad, out, grad_out, total_t, sem) = refs
        total = earlier[...]
        copy = pltpu.make_async_copy(grad, grad_out, sem)
        copy.start()
    count = len(weights) // 2
    rows, half = weights[0].shape[2:]
    cols = 2 * half
    for z in range(zs):
        pieces = tokens[:, columns_of(x, z, cols)]
        for h in range(2):
            picked = []
            for n in range(2 * ys):
                held = weights[count * (n % 2) : count * (n % 2 + 1)]
                y = n // 2
                if x and y:
                    picked.append(held[1 + 2 * (y - 1) + h][z])
                else:
                    picked.append(held[0][2 * y + h, z])
            left = jnp.concatenate(picked, axis=0)
            right = pieces[:, h * half : (h + 1) * half]
            total = total + lax.dot_general(left, right, NT, preferred_element_type=F32)
    if x == 0:
        out[...] = total
        return
    node = lax.axis_index("node")
    total_t[...] = total.reshape(total_t.shape)
    ordered = [total_t[lax.bitwise_xor(node, n)] for n in range(2 * ys)]
    out[...] = jnp.concatenate(ordered, axis=0).T.astype(BF16)
    copy.wait()


def project(tokens, near, far, grad, ys, zs):
    rows = near[0].shape[2]
    count, width = tokens.shape[0], 2 * ys * rows
    cost = pl.CostEstimate(flops=tokens.size * width, bytes_accessed=2 * tokens.size, transcendentals=0)
    earlier = pl.pallas_call(
        functools.partial(project_kernel, ys, zs, 0),
        out_shape=jax.ShapeDtypeStruct((width, count), F32),
        in_specs=[VMEM] * (1 + len(near)),
        out_specs=VMEM,
        compiler_params=PARAMS,
        cost_estimate=cost,
        name="project_near",
    )(tokens, *near)
    return pl.pallas_call(
        functools.partial(project_kernel, ys, zs, 1),
        out_shape=(jax.ShapeDtypeStruct((count, width), BF16), jax.ShapeDtypeStruct(grad.shape, F32)),
        in_specs=[VMEM] * (3 + len(far)),
        out_specs=(VMEM, ANY),
        scratch_shapes=[pltpu.VMEM((2 * ys, rows, count), F32), pltpu.SemaphoreType.DMA],
        compiler_params=PARAMS,
        cost_estimate=cost,
        name="project_far",
    )(tokens, *far, earlier, grad)


def plain_project(tokens, near, far, grad, ys, zs):
    rows, half = near[0].shape[2:]
    node, wide = lax.axis_index("node"), lax.axis_index("wide")
    pieces = tokens.reshape(tokens.shape[0], 2 * zs, 2, half)
    pieces = jnp.take(pieces, jnp.arange(2 * zs) ^ wide, axis=1)
    pieces = pieces.reshape(tokens.shape[0], zs, 2, 2, half)
    count = len(far) // 2
    weights = [
        jnp.concatenate([near[c], far[count * c], jnp.stack(far[count * c + 1 : count * (c + 1)])]) for c in range(2)
    ]
    total = []
    for n in range(2 * ys):
        part = 0.0
        for h in range(2):
            for x in range(2):
                held = weights[n % 2][place_of(h, x, n // 2, ys)]
                part = part + jnp.einsum("tzl,zrl->tr", pieces[:, :, x, h], held, preferred_element_type=F32)
        total.append(part)
    total = jnp.take(jnp.stack(total, axis=1), jnp.arange(2 * ys) ^ node, axis=1)
    return total.reshape(tokens.shape[0], -1).astype(BF16), grad


def on_device(wides, nodes, tokens, codes, scales, cotangent):
    ys, zs = nodes // 2, wides // 2
    cols, rows = codes.shape
    half = cols // 2
    aligned = half % BLOCK == 0 and rows % 16 == 0
    products, make_project = (local_products, project) if aligned else (plain_products, plain_project)
    others = range(1, ys)
    one = (zs, rows, half)
    whole = (...,)

    def core_flip(entries):
        return flip(entries, "node", 1, nodes)

    def y_flip(entries, y):
        return flip(entries, "node", 2 * y, nodes)

    def x_flip(entries):
        return flip(entries, "wide", 1, wides)

    def z_flip(entries, z):
        return flip(entries, "wide", 2 * z, wides)

    sent0, sent1, kept0, kept1, weight = products(tokens, cotangent, codes.T, scales.T, ys, zs)

    got0, got1 = core_flip(sent0), core_flip(sent1)
    held = [weight, z_flip(weight, zs // 2)]
    offsets = [0, zs // 2]
    places = [(0, ()), (1, ())]

    def pair(h, x, y):
        _, at = turn_of(h, x, y, ys)
        return [(0, (at,)), (1, (at,))]

    outs = [((ys - 1, *one), [((y - 1,), pair(1, 1, y)) for y in others])]
    outs += [(one, [(whole, pair(0, 1, y))]) for y in others]
    outs += [(one, [(whole, pair(1, 1, 0))])]
    outs += [(one, [(whole, pair(0, 0, y))]) for y in others]
    diag_x, *rest = add_up(outs, [kept0, got0], name="stage1")
    after = [diag_x]
    diag_y, side_x, side_y = rest[: ys - 1], rest[ys - 1], rest[ys:]
    diag_x = x_flip(diag_x)
    diag_y = [y_flip(d, y) for y, d in zip(others, diag_y)]
    side_x = x_flip(side_x)
    side_y = [y_flip(d, y) for y, d in zip(others, side_y)]

    step = zs // 4
    while step:
        outs = [((len(places), 2, rows, half), [((i,), [place]) for i, place in enumerate(places)])]
        (to_z,) = add_up(outs, held, after, name="widen")
        after = [to_z]
        held.append(z_flip(to_z, step))
        places = places + [(len(held) - 1, (i,)) for i in range(len(places))]
        offsets = offsets + [z ^ step for z in offsets]
        step //= 2

    outs = [(one, [(whole, pair(0, 1, 0) + [(2 + y, whole) for y in others])])]
    outs += [(one, [(whole, pair(1, 0, y) + [(2, (y - 1,))])]) for y in others]
    last_x, *last_y = add_up(outs, [kept1, got1, diag_x, *diag_y], after, name="stage2")
    after = last_x
    last_x = x_flip(last_x)
    last_y = [y_flip(d, y) for y, d in zip(others, last_y)]

    sums = [
        pair(0, 0, 0) + [(2 + y, whole) for y in others],
        pair(1, 0, 0) + [(2, whole)],
    ]
    outs = [((2, *one), [((h,), sums[h]) for h in range(2)])]
    (base,) = add_up(outs, [kept1, got1, side_x, *side_y], [after], name="sides", kind=F32)

    outs = [(one, [((z,), [(a, i + (h,))]) for z, (a, i) in zip(offsets, places)]) for h in range(2)]
    own = list(add_up(outs, held, [base], name="own"))
    on_x = [x_flip(own[0])]
    on_y = [[None, y_flip(own[1], y)] for y in others]
    on_x.append(x_flip(own[1]))
    for y in others:
        on_y[y - 1][0] = y_flip(own[0], y)
    diag = [[y_flip(on_x[0], y), x_flip(on_y[y - 1][1])] for y in others]

    arrays = [base, last_x, *last_y]
    plane = [[(0, (0,)), (1, ())], [(0, (1,))] + [(1 + y, ()) for y in others]]
    left = list(range(zs))
    sums = {(z, h): [(a, i + (z,)) for a, i in plane[h]] for z in left for h in range(2)}
    after = [own[0]]
    step = 1
    while step < zs:
        going = [z for z in left if z & step]
        left = [z for z in left if not z & step]
        outs = [((len(going), 2, rows, half), [((i, h), sums[z, h]) for i, z in enumerate(going) for h in range(2)])]
        (to_z,) = add_up(outs, arrays, after, name="plane")
        arrays = [*arrays, z_flip(to_z, step)]
        after = [to_z]
        sums = {(z, h): sums[z, h] + [(len(arrays) - 1, (i, h))] for i, z in enumerate(left) for h in range(2)}
        step *= 2
    weight_grad = finish([sums[0, 0], sums[0, 1]], arrays, tokens)

    held = own + [e for es in on_y for e in es]
    (near,) = add_up([((2 * ys, *one), [((i,), [(i, whole)]) for i in range(2 * ys)])], held, name="near")
    (side,) = add_up([((2, *one), [((h,), [(h, whole)]) for h in range(2)])], on_x, [near], name="side")
    ends = [d for ds in diag for d in ds]
    near = [near, core_flip(near)]
    far = [side, *ends, core_flip(side), *[core_flip(e) for e in ends]]
    projected, weight_grad = make_project(tokens, near, far, weight_grad, ys, zs)
    return projected, weight_grad.T


def solution(mesh):
    placed = (
        P(("wide", "node"), None),
        P("wide", "node"),
        P(None, "node"),
        P(("wide", "node"), None),
    )
    return jax.shard_map(
        functools.partial(on_device, mesh.shape["wide"], mesh.shape["node"]),
        mesh=mesh,
        in_specs=placed,
        out_specs=(P(("wide", "node"), None), P("wide", "node")),
        check_vma=False,
    )
```

```python
import functools

import jax
import jax.numpy as jnp
from jax import lax
from jax.experimental import pallas as pl
from jax.experimental.pallas import tpu as pltpu
from jax.sharding import PartitionSpec as P

BLOCK = 128
F32 = jnp.float32
BF16 = jnp.bfloat16
NT = (((1,), (1,)), ((), ()))
VMEM = pl.BlockSpec(memory_space=pltpu.VMEM)
ANY = pl.BlockSpec(memory_space=pl.ANY)
PARAMS = pltpu.CompilerParams(vmem_limit_bytes=10 << 20)


def place_of(h, x, y, ys):
    return 2 * (ys * x + y) + h


def turn_of(h, x, y, ys):
    if x and y:
        return 0, 2 * (y - 1) + h
    if (x and h) or (y and not h):
        return 0, 2 * (ys - 1) + y
    return 1, (2 + y if x or y else h)


def flip(entries, axis, offset, size):
    return lax.ppermute(entries, axis, [(i, i ^ offset) for i in range(size)])


def columns_of(x, z, cols):
    place = lax.bitwise_xor(lax.axis_index("wide"), 2 * z + x) * cols
    return pl.ds(pl.multiple_of(place, cols), cols)


def store_products(left, tokens, x, z, ys, made):
    refs = list(made.values())
    rows, half = refs[0].shape[2:]
    right = tokens[:, columns_of(x, z, 2 * half)]
    for h in range(2):
        names = [(c, y) for c in (1, 0) for y in range(ys) if (c, turn_of(h, x, y, ys)[0]) in made]
        if not names:
            continue
        picked = [left[((1 - c) * ys + y) * rows :][:rows] for c, y in names]
        picked = picked[0] if len(picked) == 1 else jnp.concatenate(picked, axis=0)
        part = jnp.dot(picked, right[:, h * half : (h + 1) * half], preferred_element_type=F32).astype(BF16)
        for i, (c, y) in enumerate(names):
            turn, at = turn_of(h, x, y, ys)
            made[c, turn][at, z] = part[i * rows : (i + 1) * rows]


def first_kernel(ys, zs, tokens, cot, sent0, left, held, cot_v, cot_t, sems):
    cols = tokens.shape[1] // (2 * zs)
    rows = sent0.shape[2]
    small = pltpu.make_async_copy(cot, cot_v, sems.at[0])
    small.start()
    order = [(x, z) for x in (1, 0) for z in range(zs)]
    copies = []
    for i, (x, z) in enumerate(order):
        place = columns_of(x, z, cols)
        copies.append(pltpu.make_async_copy(tokens.at[:, place], held.at[:, place], sems.at[1 + i]))
        copies[-1].start()
    small.wait()
    cot_t[...] = cot_v[...].astype(F32).T.astype(BF16)
    node = lax.axis_index("node")
    picked = []
    for core in (1, 0):
        for y in range(ys):
            place = lax.bitwise_xor(node, 2 * y + core) * rows
            picked.append(cot_t[pl.ds(pl.multiple_of(place, rows), rows), :])
    ordered = jnp.concatenate(picked, axis=0)
    left[...] = ordered
    for copy, (x, z) in zip(copies, order):
        copy.wait()
        store_products(ordered, held, x, z, ys, {(1, 0): sent0})


def second_kernel(ys, zs, held, left, codes, scales, sent1, kept0, kept1, weight):
    cols = codes.shape[1]
    half = cols // 2
    blocks = cols // BLOCK
    first = lax.axis_index("wide") * blocks
    shape = (scales.shape[1], blocks)
    chosen = lax.broadcasted_iota(jnp.int32, shape, 0) == first + lax.broadcasted_iota(jnp.int32, shape, 1)
    factor = jnp.dot(scales[...], chosen.astype(F32).astype(BF16), preferred_element_type=F32)
    for b in range(blocks):
        at = b * BLOCK
        piece = codes[:, at : at + BLOCK].astype(F32) * factor[:, b : b + 1]
        weight[at // half, :, at % half : at % half + BLOCK] = piece.astype(BF16)
    ordered = left[...]
    for x in (1, 0):
        for z in range(zs):
            store_products(ordered, held, x, z, ys, {(1, 1): sent1, (0, 0): kept0, (0, 1): kept1})


def local_products(tokens, cot, codes, scales, ys, zs):
    rows, cols = codes.shape
    half = cols // 2
    blocks = [jax.ShapeDtypeStruct((n, zs, rows, half), BF16) for n in (3 * ys - 2, ys + 2)]
    turned = jax.ShapeDtypeStruct(cot.shape[::-1], BF16)
    cost = pl.CostEstimate(flops=tokens.size * cot.shape[1], bytes_accessed=3 * tokens.size, transcendentals=0)
    sent0, left, held = pl.pallas_call(
        functools.partial(first_kernel, ys, zs),
        out_shape=(blocks[0], turned, jax.ShapeDtypeStruct(tokens.shape, BF16)),
        in_specs=[ANY] * 2,
        out_specs=(VMEM,) * 3,
        scratch_shapes=[
            pltpu.VMEM(cot.shape, BF16),
            pltpu.VMEM(turned.shape, BF16),
            pltpu.SemaphoreType.DMA((1 + 2 * zs,)),
        ],
        compiler_params=PARAMS,
        cost_estimate=cost,
        name="first",
    )(*[pltpu.with_memory_space_constraint(a, pltpu.HBM) for a in (tokens, cot)])
    sent1, kept0, kept1, weight = pl.pallas_call(
        functools.partial(second_kernel, ys, zs),
        out_shape=(blocks[1], *blocks, jax.ShapeDtypeStruct((2, rows, half), BF16)),
        in_specs=[VMEM] * 4,
        out_specs=(VMEM,) * 4,
        compiler_params=PARAMS,
        cost_estimate=cost,
        name="second",
    )(held, left, codes, scales)
    return sent0, sent1, kept0, kept1, weight


def plain_products(tokens, cot, codes, scales, ys, zs):
    rows, cols = codes.shape
    half = cols // 2
    node, wide = lax.axis_index("node"), lax.axis_index("wide")
    part = jnp.dot(cot.T, tokens, preferred_element_type=F32).astype(BF16)
    part = part.reshape(2 * ys, rows, 2 * zs, 2, half).transpose(3, 0, 2, 1, 4)
    part = jnp.take(part, jnp.arange(2 * ys) ^ node, axis=1)
    part = jnp.take(part, jnp.arange(2 * zs) ^ wide, axis=2)
    part = part.reshape(2, ys, 2, zs, 2, rows, half).transpose(2, 4, 1, 0, 3, 5, 6)
    part = part.reshape(2, 4 * ys, zs, rows, half)
    split = []
    for core in (1, 0):
        named = {turn_of(h, x, y, ys): part[core, place_of(h, x, y, ys)] for h in range(2) for x in range(2) for y in range(ys)}
        for turn, count in enumerate((3 * ys - 2, ys + 2)):
            split.append(jnp.stack([named[turn, i] for i in range(count)]))
    index = (wide * cols + jnp.arange(cols)) // BLOCK
    factor = jnp.take(scales, index, axis=1).astype(F32)
    weight = (codes.astype(F32) * factor).astype(BF16)
    weight = weight.reshape(rows, 2, half).transpose(1, 0, 2)
    return *split, weight


def add_up(outs, arrays, after=(), name="add_up", kind=BF16):
    shapes = [jax.ShapeDtypeStruct(shape, kind) for shape, _ in outs]
    rows, half = arrays[0].shape[-2:]
    if half % BLOCK or rows % 16:
        results = []
        for shape, places in outs:
            result = jnp.zeros(shape, kind)
            for at, terms in places:
                total = sum(arrays[a][i].astype(F32) for a, i in terms)
                result = result.at[at].set(total.astype(kind))
            results.append(result)
        return results

    def kernel(*refs):
        given, made = refs[: len(arrays)], refs[len(arrays) + len(after) :]
        for out, (_, places) in zip(made, outs):
            for at, terms in places:
                terms = [given[a][i] for a, i in terms]
                if len(terms) > 1:
                    terms = [sum(t.astype(F32) for t in terms).astype(kind)]
                out[at] = terms[0]

    return pl.pallas_call(
        kernel,
        out_shape=shapes,
        in_specs=[VMEM] * len(arrays) + [ANY] * len(after),
        out_specs=[VMEM] * len(outs),
        compiler_params=PARAMS,
        name=name,
    )(*arrays, *after)


def finish(sums, arrays, after):
    rows, half = arrays[0].shape[-2:]

    def total(given, h):
        return sum(given[a][i].astype(F32) for a, i in sums[h])

    if half % BLOCK or rows % 16:
        return jnp.concatenate([total(arrays, h) for h in range(2)], axis=1)

    def kernel(*refs):
        for h in range(2):
            refs[-1][:, h * half : (h + 1) * half] = total(refs[:-2], h)

    return pl.pallas_call(
        kernel,
        out_shape=jax.ShapeDtypeStruct((rows, 2 * half), F32),
        in_specs=[VMEM] * len(arrays) + [ANY],
        out_specs=VMEM,
        compiler_params=PARAMS,
        cost_estimate=pl.CostEstimate(flops=4 * 10**10, bytes_accessed=1, transcendentals=0),
        name="finish",
    )(*arrays, after)


def project_kernel(ys, zs, x, tokens, *refs):
    if x == 0:
        (*weights, out) = refs
        total = 0.0
    else:
        (earlier, grad, *weights, out, grad_out, total_t, sem) = refs
        total = earlier[...]
        copy = pltpu.make_async_copy(grad, grad_out, sem)
        copy.start()
    count = len(weights) // 2
    rows, half = weights[0].shape[2:]
    cols = 2 * half
    for z in range(zs):
        pieces = tokens[:, columns_of(x, z, cols)]
        for h in range(2):
            picked = []
            for n in range(2 * ys):
                held = weights[count * (n % 2) : count * (n % 2 + 1)]
                y = n // 2
                if x and y:
                    picked.append(held[1 + 2 * (y - 1) + h][z])
                else:
                    picked.append(held[0][2 * y + h, z])
            left = jnp.concatenate(picked, axis=0)
            right = pieces[:, h * half : (h + 1) * half]
            total = total + lax.dot_general(left, right, NT, preferred_element_type=F32)
    if x == 0:
        out[...] = total
        return
    node = lax.axis_index("node")
    total_t[...] = total.reshape(total_t.shape)
    ordered = [total_t[lax.bitwise_xor(node, n)] for n in range(2 * ys)]
    out[...] = jnp.concatenate(ordered, axis=0).T.astype(BF16)
    copy.wait()


def project(tokens, near, far, grad, ys, zs):
    rows = near[0].shape[2]
    count, width = tokens.shape[0], 2 * ys * rows
    cost = pl.CostEstimate(flops=tokens.size * width, bytes_accessed=2 * tokens.size, transcendentals=0)
    earlier = pl.pallas_call(
        functools.partial(project_kernel, ys, zs, 0),
        out_shape=jax.ShapeDtypeStruct((width, count), F32),
        in_specs=[VMEM] * (1 + len(near)),
        out_specs=VMEM,
        compiler_params=PARAMS,
        cost_estimate=cost,
        name="project_near",
    )(tokens, *near)
    return pl.pallas_call(
        functools.partial(project_kernel, ys, zs, 1),
        out_shape=(jax.ShapeDtypeStruct((count, width), BF16), jax.ShapeDtypeStruct(grad.shape, F32)),
        in_specs=[VMEM] * (3 + len(far)),
        out_specs=(VMEM, ANY),
        scratch_shapes=[pltpu.VMEM((2 * ys, rows, count), F32), pltpu.SemaphoreType.DMA],
        compiler_params=PARAMS,
        cost_estimate=cost,
        name="project_far",
    )(tokens, earlier, grad, *far)


def plain_project(tokens, near, far, grad, ys, zs):
    rows, half = near[0].shape[2:]
    node, wide = lax.axis_index("node"), lax.axis_index("wide")
    pieces = tokens.reshape(tokens.shape[0], 2 * zs, 2, half)
    pieces = jnp.take(pieces, jnp.arange(2 * zs) ^ wide, axis=1)
    pieces = pieces.reshape(tokens.shape[0], zs, 2, 2, half)
    count = len(far) // 2
    weights = [
        jnp.concatenate([near[c], far[count * c], jnp.stack(far[count * c + 1 : count * (c + 1)])]) for c in range(2)
    ]
    total = []
    for n in range(2 * ys):
        part = 0.0
        for h in range(2):
            for x in range(2):
                held = weights[n % 2][place_of(h, x, n // 2, ys)]
                part = part + jnp.einsum("tzl,zrl->tr", pieces[:, :, x, h], held, preferred_element_type=F32)
        total.append(part)
    total = jnp.take(jnp.stack(total, axis=1), jnp.arange(2 * ys) ^ node, axis=1)
    return total.reshape(tokens.shape[0], -1).astype(BF16), grad


def on_device(wides, nodes, tokens, codes, scales, cotangent):
    ys, zs = nodes // 2, wides // 2
    cols, rows = codes.shape
    half = cols // 2
    aligned = half % BLOCK == 0 and rows % 16 == 0
    products, make_project = (local_products, project) if aligned else (plain_products, plain_project)
    others = range(1, ys)
    one = (zs, rows, half)
    whole = (...,)

    def core_flip(entries):
        return flip(entries, "node", 1, nodes)

    def y_flip(entries, y):
        return flip(entries, "node", 2 * y, nodes)

    def x_flip(entries):
        return flip(entries, "wide", 1, wides)

    def z_flip(entries, z):
        return flip(entries, "wide", 2 * z, wides)

    sent0, sent1, kept0, kept1, weight = products(tokens, cotangent, codes.T, scales.T, ys, zs)

    got0, got1 = core_flip(sent0), core_flip(sent1)
    held = [weight, z_flip(weight, zs // 2)]
    offsets = [0, zs // 2]
    places = [(0, ()), (1, ())]

    def pair(h, x, y):
        _, at = turn_of(h, x, y, ys)
        return [(0, (at,)), (1, (at,))]

    outs = [((ys - 1, *one), [((y - 1,), pair(1, 1, y)) for y in others])]
    outs += [(one, [(whole, pair(0, 1, y))]) for y in others]
    outs += [(one, [(whole, pair(0, 0, y))]) for y in others]
    outs += [(one, [(whole, pair(1, 1, 0))])]
    diag_x, *rest = add_up(outs, [kept0, got0], name="stage1")
    after = [diag_x]
    diag_y, side_y, side_x = rest[: ys - 1], rest[ys - 1 : -1], rest[-1]
    diag_x = x_flip(diag_x)
    diag_y = [y_flip(d, y) for y, d in zip(others, diag_y)]
    side_y = [y_flip(d, y) for y, d in zip(others, side_y)]
    side_x = x_flip(side_x)

    step = zs // 4
    while step:
        outs = [((len(places), 2, rows, half), [((i,), [place]) for i, place in enumerate(places)])]
        (to_z,) = add_up(outs, held, after, name="widen")
        after = [to_z]
        held.append(z_flip(to_z, step))
        places = places + [(len(held) - 1, (i,)) for i in range(len(places))]
        offsets = offsets + [z ^ step for z in offsets]
        step //= 2

    outs = [(one, [(whole, pair(0, 1, 0) + [(2 + y, whole) for y in others])])]
    outs += [(one, [(whole, pair(1, 0, y) + [(2, (y - 1,))])]) for y in others]
    last_x, *last_y = add_up(outs, [kept1, got1, diag_x, *diag_y], after, name="stage2")
    after = last_x
    last_x = x_flip(last_x)
    last_y = [y_flip(d, y) for y, d in zip(others, last_y)]

    sums = [
        pair(0, 0, 0) + [(1 + y, whole) for y in others],
        pair(1, 0, 0) + [(1 + ys, whole)],
    ]
    outs = [((2, *one), [((h,), sums[h]) for h in range(2)])]
    (base,) = add_up(outs, [kept1, got1, *side_y, side_x], [after], name="sides", kind=F32)

    outs = [(one, [((z,), [(a, i + (h,))]) for z, (a, i) in zip(offsets, places)]) for h in range(2)]
    own = list(add_up(outs, held, [base], name="own"))
    on_x = [x_flip(own[0])]
    on_y = [[None, y_flip(own[1], y)] for y in others]
    on_x.append(x_flip(own[1]))
    for y in others:
        on_y[y - 1][0] = y_flip(own[0], y)
    diag = [[y_flip(on_x[0], y), x_flip(on_y[y - 1][1])] for y in others]

    arrays = [base, last_x, *last_y]
    plane = [[(0, (0,)), (1, ())], [(0, (1,))] + [(1 + y, ()) for y in others]]
    left = list(range(zs))
    sums = {(z, h): [(a, i + (z,)) for a, i in plane[h]] for z in left for h in range(2)}
    after = [own[0]]
    step = 1
    while step < zs:
        going = [z for z in left if z & step]
        left = [z for z in left if not z & step]
        outs = [((len(going), 2, rows, half), [((i, h), sums[z, h]) for i, z in enumerate(going) for h in range(2)])]
        (to_z,) = add_up(outs, arrays, after, name="plane")
        arrays = [*arrays, z_flip(to_z, step)]
        after = [to_z]
        sums = {(z, h): sums[z, h] + [(len(arrays) - 1, (i, h))] for i, z in enumerate(left) for h in range(2)}
        step *= 2
    weight_grad = finish([sums[0, 0], sums[0, 1]], arrays, tokens)

    held = own + [e for es in on_y for e in es]
    (near,) = add_up([((2 * ys, *one), [((i,), [(i, whole)]) for i in range(2 * ys)])], held, name="near")
    (side,) = add_up([((2, *one), [((h,), [(h, whole)]) for h in range(2)])], on_x, [near], name="side")
    ends = [d for ds in diag for d in ds]
    near = [near, core_flip(near)]
    far = [side, *ends, core_flip(side), *[core_flip(e) for e in ends]]
    projected, weight_grad = make_project(tokens, near, far, weight_grad, ys, zs)
    return projected, weight_grad.T


def solution(mesh):
    placed = (
        P(("wide", "node"), None),
        P("wide", "node"),
        P(None, "node"),
        P(("wide", "node"), None),
    )
    return jax.shard_map(
        functools.partial(on_device, mesh.shape["wide"], mesh.shape["node"]),
        mesh=mesh,
        in_specs=placed,
        out_specs=(P(("wide", "node"), None), P("wide", "node")),
        check_vma=False,
    )
```
